128 devices in a mesh: ctx: 16 (over y, x), head: 8 (over z, core).
Axes of the slice: x: 4, y: 4, z: 4, core: 2. Of those that a mesh axis runs over, the one named last changes fastest.
Arguments:
- queries: bfloat16 [1024, 64, 192], P(('ctx', 'head')), may hold values from -24 to 24
- latent_cache: bfloat16 [8192, 576], P('ctx'), may hold values from -8 to 8
- absorb_key: bfloat16 [64, 128, 512], P('head'), may hold values from -0.5 to 0.5
- absorb_value: bfloat16 [64, 512, 128], P('head'), may hold values from -6 to 6
- out_proj: bfloat16 [8192, 7168], P('head'), may hold values from -0.009765625 to 0.009765625
- residual: bfloat16 [1024, 7168], P(('ctx', 'head')), may hold values from -0.8984375 to 0.8984375
- norm_gain: float32 [7168], replicated, may hold values from 0.25 to 1.75
- routes: int32 [1024, 8], P(('ctx', 'head')), may hold values from 0 to 15, all different within a row; in each aligned block of 8 rows (0 to 7, 8 to 15, ...) at most 6 rows name the same one
- route_score: float32 [1024, 8], P(('ctx', 'head')), may hold values from 0.5 to 1
- response_doc: int32 [1024], replicated, may hold values from 0 to 7, never falling along the last dimension, each value on 1 to 512 neighbouring positions
- expert_gate: bfloat16 [16, 7168, 1024], P('ctx', None, 'head'), may hold values from -0.0625 to 0.0625
- expert_up: bfloat16 [16, 7168, 1024], P('ctx', None, 'head'), may hold values from -0.0625 to 0.0625
- expert_down: bfloat16 [16, 1024, 7168], P('ctx', 'head'), may hold values from -0.75 to 0.75
Outputs:
- layer_out: bfloat16 [1024, 7168], P(('ctx', 'head'))
The draws below stay inside these ranges and needn't reach their ends.
Inputs may be any that keep to these rules, and one draw needn't show every extreme that they name: `routes`: each row names 8 different experts. In the rows of one device (8 aligned rows) no expert is named by more than 6 rows, a bound that some block reaches. `response_doc`: never falling; each response has 1 to 512 tokens, one exactly 512.
All inputs are finite; a program needn't handle non-finite values.
Results may differ from the reference program's by a relative error of at most 0.03.
Values may be sent and summed in bfloat16 or wider, within the bound.
No kernel may reach another device: no remote copies, remote signals or barrier semaphores. Data moves between devices by JAX's collectives and lax.ppermute only.
A program may use at most 128 MiB of HBM per device.

```python
import math
import jax
import jax.numpy as jnp
import numpy as np
from jax import lax

D = 7168
HEADS = 64
NOPE = 128
ROPE = 64
LAT = 512
VDIM = 128
FF_EXP = 1024
EXPERTS = 16
TOP = 8
RESP = 1024
NRESP = 8
CTX = 8192
PROMPT = 7168
TOK_DEV = 8
CAP = 6
N_CTX = 16
N_HEAD = 8


def draw_queries(key, part):
    key = jax.random.fold_in(key, 3)
    first = jax.random.fold_in(key, 0)
    values = jnp.clip(jax.random.normal(first, (RESP, HEADS, NOPE + ROPE), jnp.float32), -6.0, 6.0)
    return values.astype(jnp.bfloat16)


def draw_latent_cache(key, part):
    key = jax.random.fold_in(key, 5)
    first = jax.random.fold_in(key, 0)
    values = jnp.clip(jax.random.normal(first, (CTX, LAT + ROPE), jnp.float32), -6.0, 6.0)
    return values.astype(jnp.bfloat16)


def shard_levels(own_key, shape, pieces, low, high):
    def one(position, parts):
        heights = jax.random.uniform(jax.random.fold_in(jax.random.fold_in(own_key, 6), position), (parts,), jnp.float32, low / len(pieces), high / len(pieces))
        return jnp.repeat(jnp.exp(heights), shape[position] // parts).reshape((-1,) + (1,) * (len(shape) - position - 1))

    factor_of = one(*pieces[0])
    for cut in pieces[1:]:
        factor_of = factor_of * one(*cut)
    return factor_of


def length_profile(number_of, total, bound, slope):
    loads = [(1 << 20) // math.isqrt(standing ** slope) + 1 for standing in range(2, number_of + 1)]
    surplus, holding = total - bound - (number_of - 1), [1] * (number_of - 1)
    while surplus > 0:
        free = [i for i in range(number_of - 1) if holding[i] < bound]
        mass, budget = sum([loads[i] for i in free]), surplus
        for i in free:
            extra = min(bound - holding[i], max(1, budget * loads[i] // mass), surplus)
            holding[i] = holding[i] + extra
            surplus = surplus - extra
    return np.array([bound] + holding)


def ragged(own_key, count, total, reach, slope):
    if count == 2:
        one = jax.random.randint(own_key, (), max(1, total - reach), min(reach, total - 1) + 1)
        return jnp.stack([one, total - one])
    sizes = jnp.asarray(length_profile(count, total, reach, slope), jnp.int32)
    couples = (count - 1) // 2
    source_of, sink = sizes[1:1 + 2 * couples:2], sizes[2:2 + 2 * couples:2]
    room = jnp.minimum(source_of - 1, reach - sink)
    shifted = jax.random.randint(jax.random.fold_in(own_key, 1), (couples,), 0, 1 << 20) % (room + 1)
    sizes = sizes.at[1:1 + 2 * couples:2].set(source_of - shifted).at[2:2 + 2 * couples:2].set(sink + shifted)
    return sizes[jax.random.permutation(jax.random.fold_in(own_key, 2), count)]


def assign_block(key, own, number, rows, number_of, top, bound, lean):
    order = jax.random.permutation(key, number_of)
    heavy_load, common = shares(number_of, rows * top, bound, lean, True), shares(number_of, rows * top, bound, lean, False)
    places = jnp.arange(number_of)

    def named(tallies, turn):
        used = int((tallies > 0).sum())
        fixed = max(1, used // 4)
        passed = fixed + (places - fixed + turn * (used - fixed)) % max(1, number_of - fixed)
        return jnp.zeros((number_of,), jnp.int32).at[order[jnp.where(places < fixed, places, passed)]].set(jnp.asarray(tallies, jnp.int32))

    tallies = jnp.where(number % 4 == 0, named(heavy_load, number // 4), named(common, number - number // 4 - 1))
    mixed = jax.random.permutation(jax.random.fold_in(own, 3), number_of)
    giver, taker = mixed[0:number_of // 2 * 2:2], mixed[1:number_of // 2 * 2:2]
    slack = jnp.minimum(tallies[giver] - 1, bound - tallies[taker]) // 2
    slack = jnp.where((giver == order[0]) | (taker == order[0]) | (tallies[taker] == 0), 0, jnp.maximum(slack, 0))
    passed = jax.random.randint(jax.random.fold_in(own, 4), (number_of // 2,), 0, 1 << 20) % (slack + 1)
    tallies = tallies.at[giver].add(-passed).at[taker].add(passed)
    labels = jnp.searchsorted(jnp.cumsum(tallies), jnp.arange(rows * top), side="right").astype(jnp.int32)
    grid = labels.reshape(top, rows).T
    grid = grid[jax.random.permutation(jax.random.fold_in(own, 1), rows)]
    turn = jax.random.randint(jax.random.fold_in(own, 2), (rows, 1), 0, top)
    return jnp.take_along_axis(grid, (jnp.arange(top)[None, :] + turn) % top, axis=1)


def shares(number_of, total, bound, skew, full):
    loads = [(1 << 20) // math.isqrt(grade ** skew) + 1 for grade in range(1, number_of + 1)]
    largest = bound if full else min(bound, max(-(-total // number_of), total * loads[0] // sum(loads)))
    least = 1 if total - largest >= number_of - 1 else 0
    counts, rest = [largest] + [least] * (number_of - 1), total - largest - least * (number_of - 1)
    while rest > 0:
        movable = [i for i in range(1, number_of) if counts[i] < largest] or [i for i in range(1, number_of) if counts[i] < bound]
        mass, left = sum([loads[i] for i in movable]), rest
        for i in movable:
            more = min(bound - counts[i], max(1, left * loads[i] // mass), rest)
            counts[i] = counts[i] + more
            rest = rest - more
    return np.array(counts)


def bell_draw(rng, extent, width, limit, cuts=(), held_as=jnp.bfloat16):
    level = shard_levels(rng, extent, cuts, -0.22, 0.18) if cuts else 1.0
    values = jax.random.normal(rng, extent, jnp.float32) * width * level
    return jnp.minimum(jnp.maximum(values, -limit), limit).astype(held_as)


def setup_inputs(seed: int = 0) -> dict:
    streams_of = jax.random.split(jax.random.key(seed), 14)
    queries = draw_queries(jax.random.fold_in(streams_of[13], 71), 0)
    latent_cache = draw_latent_cache(jax.random.fold_in(streams_of[13], 71), 0)
    absorb_key = bell_draw(streams_of[2], (HEADS, NOPE, LAT), NOPE ** -0.5, 0.5, ((0, 8),))
    absorb_value = bell_draw(streams_of[3], (HEADS, LAT, VDIM), 1.0, 6.0, ((0, 8),))
    out_proj = bell_draw(streams_of[4], (HEADS * VDIM, D), (50 * HEADS * VDIM) ** -0.5, 0.009765625, ((0, 8),))
    residual = bell_draw(streams_of[5], (RESP, D), 0.15, 0.8984375, ((0, 128),))
    norm_gain = jnp.clip(1.0 + 0.15 * jax.random.normal(streams_of[6], (D,), jnp.float32), 0.25, 1.75)
    routes_keys = jax.random.split(jax.random.fold_in(streams_of[7], 1), RESP // TOK_DEV)
    routes_turns = jax.random.permutation(jax.random.fold_in(streams_of[7], 3), RESP // TOK_DEV)
    routes = jax.vmap(lambda own, number: assign_block(jax.random.fold_in(streams_of[7], 2), own, number, TOK_DEV, EXPERTS, TOP, CAP, 2))(routes_keys, routes_turns).reshape((RESP, TOP))
    route_score = jnp.clip(0.5 + 0.5 * jax.random.uniform(streams_of[8], (RESP, TOP), jnp.float32) ** shard_levels(streams_of[8], (RESP, TOP), ((0, 128),), -0.2, 0.2), 0.5, 1.0)
    response_doc = jnp.searchsorted(jnp.cumsum(ragged(streams_of[9], NRESP, RESP, RESP // 2, 1)), jnp.arange(RESP), side="right").astype(jnp.int32)
    expert_gate = bell_draw(streams_of[10], (EXPERTS, D, FF_EXP), D ** -0.5, 0.0625, ((0, 16), (2, 8)))
    expert_up = bell_draw(streams_of[11], (EXPERTS, D, FF_EXP), D ** -0.5, 0.0625, ((0, 16), (2, 8)))
    expert_down = bell_draw(streams_of[12], (EXPERTS, FF_EXP, D), (FF_EXP // 16) ** -0.5, 0.75, ((0, 16), (1, 8)))
    return {"queries": queries, "latent_cache": latent_cache, "absorb_key": absorb_key, "absorb_value": absorb_value, "out_proj": out_proj, "residual": residual, "norm_gain": norm_gain, "routes": routes, "route_score": route_score, "response_doc": response_doc, "expert_gate": expert_gate, "expert_up": expert_up, "expert_down": expert_down}


def visible_mask(row_pos, row_doc, key_pos, response_doc):
    key_doc = jnp.take(response_doc, jnp.clip(key_pos - PROMPT, 0, RESP - 1))
    inside = (key_doc[None, :] == row_doc[:, None]) & (key_pos[None, :] <= row_pos[:, None])
    return (key_pos[None, :] < PROMPT) | inside

def reference(queries, latent_cache, absorb_key, absorb_value, out_proj, residual, norm_gain, routes, route_score, response_doc, expert_gate, expert_up, expert_down):
    score_scale = (NOPE + ROPE) ** (-0.5)
    query_nope = queries[:, :, :NOPE].astype(jnp.float32)
    query_latent = jnp.einsum('thn,hnl->thl', query_nope, absorb_key.astype(jnp.float32)).astype(jnp.bfloat16)
    query_full = jnp.concatenate([query_latent, queries[:, :, NOPE:]], axis=2)
    row_pos = PROMPT + jnp.arange(RESP, dtype=jnp.int32)
    key_pos = jnp.arange(CTX, dtype=jnp.int32)
    visible = visible_mask(row_pos, response_doc, key_pos, response_doc)
    values = latent_cache[:, :LAT]

    def one_head(query_head):
        scores = jnp.dot(query_head, latent_cache.T, preferred_element_type=jnp.float32) * score_scale
        scores = jnp.where(visible, scores, -1e+30)
        row_max = lax.optimization_barrier(jnp.max(scores, axis=1, keepdims=True))
        exp_scores = jnp.where(visible, jnp.exp(scores - row_max), 0.0)
        row_total = lax.optimization_barrier(jnp.sum(exp_scores, axis=1, keepdims=True))
        mixed = jnp.dot(exp_scores.astype(jnp.bfloat16), values, preferred_element_type=jnp.float32)
        return (mixed / row_total).astype(jnp.bfloat16)
    out_latent = lax.map(one_head, jnp.swapaxes(query_full, 0, 1))
    head_out = jnp.einsum('htl,hlv->thv', out_latent.astype(jnp.float32), absorb_value.astype(jnp.float32)).astype(jnp.bfloat16)
    attended = jnp.dot(head_out.reshape(RESP, HEADS * VDIM), out_proj, preferred_element_type=jnp.float32)
    hidden_state = residual.astype(jnp.float32) + attended
    mean_square = lax.optimization_barrier(jnp.mean(hidden_state * hidden_state, axis=1, keepdims=True))
    normed = (hidden_state * lax.rsqrt(mean_square + 1e-06) * norm_gain.astype(jnp.float32)).astype(jnp.bfloat16)
    tok_dev = RESP // (N_CTX * N_HEAD)
    capacity = max(2, tok_dev * 3 // 4)
    block_count = RESP // tok_dev
    flat_exp = routes.reshape(-1).astype(jnp.int32)
    onehot = (flat_exp[:, None] == jnp.arange(EXPERTS, dtype=jnp.int32)[None, :]).astype(jnp.int32)
    onehot_blocks = onehot.reshape(block_count, tok_dev * TOP, EXPERTS)
    before = jnp.cumsum(onehot_blocks, axis=1) - onehot_blocks
    slot_index = lax.optimization_barrier(jnp.sum(before * onehot_blocks, axis=2)).reshape(-1).astype(jnp.int32)
    block_id = (jnp.arange(RESP * TOP, dtype=jnp.int32) // (tok_dev * TOP)).astype(jnp.int32)
    dest_row = (flat_exp * (block_count * capacity) + block_id * capacity + slot_index).astype(jnp.int32)
    source = jnp.repeat(normed, TOP, axis=0)
    buffer = jnp.zeros((EXPERTS * block_count * capacity, D), jnp.bfloat16).at[dest_row].set(source)
    buffer = buffer.reshape(EXPERTS, block_count * capacity, D)
    slice_width = FF_EXP // N_HEAD

    def run_expert(operands):
        rows, gate_w, up_w, down_w = operands
        row_total = jnp.zeros((block_count * capacity, D), jnp.float32)
        for slice_idx in range(N_HEAD):
            low = slice_idx * slice_width
            gate_act = jnp.dot(rows, gate_w[:, low:low + slice_width], preferred_element_type=jnp.float32)
            up_act = jnp.dot(rows, up_w[:, low:low + slice_width], preferred_element_type=jnp.float32)
            inner_act = (jax.nn.silu(gate_act) * up_act).astype(jnp.bfloat16)
            part_value = jnp.dot(inner_act, down_w[low:low + slice_width, :], preferred_element_type=jnp.float32)
            part_value = lax.optimization_barrier(part_value.astype(jnp.bfloat16))
            row_total = row_total + part_value.astype(jnp.float32)
        return row_total
    outputs = lax.map(run_expert, (buffer, expert_gate, expert_up, expert_down))
    outputs = outputs.reshape(EXPERTS * block_count * capacity, D)
    picked = jnp.take(outputs, dest_row, axis=0).reshape(RESP, TOP, D)
    weight = 2.5 * route_score / lax.optimization_barrier(jnp.sum(route_score, axis=1, keepdims=True))
    expert_mix = lax.optimization_barrier(jnp.sum(weight[:, :, None] * picked, axis=1))
    return (hidden_state + expert_mix).astype(jnp.bfloat16)
```

```python
import functools

import jax
import jax.numpy as jnp
from jax import lax
from jax.experimental import pallas as pl
from jax.experimental.pallas import tpu as pltpu
from jax.sharding import Mesh
from jax.sharding import PartitionSpec as P

D = 7168
NOPE = 128
ROPE = 64
LAT = 512
VDIM = 128
EXPERTS = 16
TOP = 8
RESP = 1024
PROMPT = 7168
NX = 4
NY = 4
NZ = 4
GRP = 8
BLK = 8
CAP = 6
KEYS = 2048
HALF = 256
ROWS = 256
CHUNK = D // NZ
SLOTS = NZ * CAP
EROWS = 16 * SLOTS
LOG2E = 1.4426950408889634
BF = jnp.bfloat16
F32 = jnp.float32
HIDE = -1e30


def shift(a, axis, n, d):
    return lax.ppermute(a, axis, [(i, (i + d) % n) for i in range(n)])


def split3(v):
    hi = v.astype(BF).astype(F32)
    mid = (v - hi).astype(BF).astype(F32)
    low = (v - hi - mid).astype(BF).astype(F32)
    return hi, mid, low


def attention_kernel(
    pos_ref, q_ref, first_ref, last_ref, c0, c1, c2, c3, s1, s2, s3, ak_ref, av_ref, o_ref, kv, rp, st
):
    h = pl.program_id(0)

    @pl.when(h == 0)
    def _():
        kv[pl.ds(pl.multiple_of(pos_ref[0], HALF), 2 * HALF), :] = c0[...]
        for i, piece in enumerate((c1, c2, c3, s1, s2, s3)):
            kv[pl.ds(pl.multiple_of(pos_ref[1 + i], HALF), HALF), :] = piece[...]
        r = kv[:, LAT:]
        rp[...] = jnp.concatenate([r, r], axis=1)
        st[...] = jnp.zeros_like(st)

    nope = q_ref[:, pl.ds(pl.multiple_of(h * NOPE, NOPE), NOPE)]
    q_lat = jnp.dot(nope, ak_ref[0], preferred_element_type=F32).astype(BF)
    pair = q_ref[:, pl.ds(pl.multiple_of(GRP * NOPE + (h // 2) * 128, 128), 128)].astype(F32)
    lane = lax.broadcasted_iota(jnp.int32, (ROWS, 128), 1)
    rope = jnp.where(lane // ROPE == h % 2, pair, 0.0).astype(BF)
    nt = (((1,), (1,)), ((), ()))
    step = 512
    parts = []
    for j in range(0, KEYS, step):
        s = lax.dot_general(q_lat, kv[j : j + step, :LAT], nt, preferred_element_type=F32)
        s = s + lax.dot_general(rope, rp[j : j + step, :], nt, preferred_element_type=F32)
        if j >= KEYS // 2:
            col = lax.broadcasted_iota(jnp.int32, (ROWS, step), 1) + (j - KEYS // 2)
            s = jnp.where((col >= first_ref[...]) & (col <= last_ref[...]), s, HIDE)
        parts.append(s)
    top = jnp.max(parts[0], axis=1, keepdims=True)
    for s in parts[1:]:
        top = jnp.maximum(top, jnp.max(s, axis=1, keepdims=True))
    scale = LOG2E * (NOPE + ROPE) ** (-0.5)
    total = jnp.zeros((ROWS, 1), F32)
    acc = jnp.zeros((ROWS, LAT), F32)
    for i, s in enumerate(parts):
        p = jnp.exp2((s - top) * scale)
        total = total + jnp.sum(p, axis=1, keepdims=True)
        acc = acc + jnp.dot(p.astype(BF), kv[i * step : (i + 1) * step, :LAT], preferred_element_type=F32)
    lat = (acc / total).astype(BF)
    o_ref[:, pl.ds(pl.multiple_of(h * VDIM, VDIM), VDIM)] = jnp.dot(
        lat, av_ref[0], preferred_element_type=F32
    ).astype(BF)
    add = jnp.zeros((ROWS, 128), F32)
    for i, v in enumerate(split3(top) + split3(total)):
        add = add + jnp.where(lane == i * GRP + h, v, 0.0)
    st[...] += add

    @pl.when(h == GRP - 1)
    def _():
        o_ref[:, GRP * VDIM :] = st[...].astype(BF)


def attention(place, q, first, last, pieces, absorb_key, absorb_value):
    whole = lambda a: pl.BlockSpec(a.shape, lambda h: (0,) * a.ndim)
    return pl.pallas_call(
        attention_kernel,
        grid=(GRP,),
        out_shape=jax.ShapeDtypeStruct((ROWS, GRP * VDIM + 128), BF),
        in_specs=[pl.BlockSpec(memory_space=pltpu.SMEM), whole(q), whole(first), whole(last)]
        + [whole(p) for p in pieces]
        + [
            pl.BlockSpec((1, NOPE, LAT), lambda h: (h, 0, 0)),
            pl.BlockSpec((1, LAT, VDIM), lambda h: (h, 0, 0)),
        ],
        out_specs=pl.BlockSpec((ROWS, GRP * VDIM + 128), lambda h: (0, 0)),
        scratch_shapes=[
            pltpu.VMEM((KEYS, LAT + ROPE), BF),
            pltpu.VMEM((KEYS, 2 * ROPE), BF),
            pltpu.VMEM((ROWS, 128), F32),
        ],
        compiler_params=pltpu.CompilerParams(vmem_limit_bytes=40 * 2**20),
        cost_estimate=pl.CostEstimate(flops=9 * 10**9, bytes_accessed=6 * 10**6, transcendentals=4 * 10**6),
        name="attention",
    )(place, q, first, last, *pieces, absorb_key, absorb_value)


def gate_up_kernel(z_ref, x_ref, *refs):
    pieces, (o_ref, w, sem) = refs[:8], refs[8:]
    copies = [pltpu.make_async_copy(p, w.at[i], sem.at[i]) for i, p in enumerate(pieces)]
    for c in copies:
        c.start()
    for i, c in enumerate(copies):
        c.wait()
        d, k = i // 2, i % 2
        part = jnp.dot(x_ref[...], w[i], preferred_element_type=F32).astype(BF)
        o_ref[lax.rem(z_ref[0] + NZ - d, NZ), :, k * 256 : (k + 1) * 256] = part


def gate_up(z, x, pieces):
    return pl.pallas_call(
        gate_up_kernel,
        out_shape=jax.ShapeDtypeStruct((NZ, EROWS, 512), BF),
        in_specs=[pl.BlockSpec(memory_space=pltpu.SMEM), pl.BlockSpec(memory_space=pltpu.VMEM)]
        + [pl.BlockSpec(memory_space=pl.ANY)] * 8,
        out_specs=pl.BlockSpec(memory_space=pltpu.VMEM),
        scratch_shapes=[pltpu.VMEM((8, CHUNK, 256), BF), pltpu.SemaphoreType.DMA((8,))],
        compiler_params=pltpu.CompilerParams(vmem_limit_bytes=40 * 2**20),
        cost_estimate=pl.CostEstimate(flops=3 * 10**9, bytes_accessed=10 * 10**6, transcendentals=0),
        name="gate_up",
    )(z, x, *pieces)


def down_kernel(i0, i1, i2, i3, *refs):
    pieces, (o_ref, w, sem) = refs[:8], refs[8:]
    copies = [
        pltpu.make_async_copy(p, w.at[pl.ds(i * 128, 128)], sem.at[i]) for i, p in enumerate(pieces)
    ]
    for c in copies:
        c.start()
    inner = jnp.concatenate([i0[...], i1[...], i2[...], i3[...]], axis=1)
    for c in copies:
        c.wait()
    for j in range(0, CHUNK, 256):
        o_ref[:, j : j + 256] = jnp.dot(inner, w[:, j : j + 256], preferred_element_type=F32).astype(BF)


def down(inners, pieces):
    return pl.pallas_call(
        down_kernel,
        out_shape=jax.ShapeDtypeStruct((EROWS, CHUNK), BF),
        in_specs=[pl.BlockSpec(memory_space=pltpu.VMEM)] * 4 + [pl.BlockSpec(memory_space=pl.ANY)] * 8,
        out_specs=pl.BlockSpec(memory_space=pltpu.VMEM),
        scratch_shapes=[pltpu.VMEM((1024, CHUNK), BF), pltpu.SemaphoreType.DMA((8,))],
        compiler_params=pltpu.CompilerParams(vmem_limit_bytes=40 * 2**20),
        cost_estimate=pl.CostEstimate(flops=14 * 10**8, bytes_accessed=6 * 10**6, transcendentals=0),
        name="down",
    )(*inners, *pieces)


def after(arrays, token):
    out = lax.optimization_barrier(tuple(arrays) + (token,))
    return out[:-1]


def absolute(rel, z):
    line = jnp.stack([rel[3], rel[2], rel[1], rel[0], rel[3], rel[2], rel[1]])
    return lax.dynamic_slice_in_dim(line, 3 - z, NZ, axis=0)


def shards(
    queries,
    latent_cache,
    absorb_key,
    absorb_value,
    out_proj,
    residual,
    norm_gain,
    routes,
    route_score,
    response_doc,
    expert_gate,
    expert_up,
    expert_down,
):
    x, y, z, k = (lax.axis_index(a) for a in ("x", "y", "z", "core"))

    with jax.named_scope("cache_gather"):
        half = lax.dynamic_slice_in_dim(latent_cache, k * HALF, HALF, axis=0)
        mine = [shift(half, "x", NX, d) for d in range(1, NX)]
        other = [shift(m, "core", 2, 1) for m in mine]

    with jax.named_scope("query_exchange"):
        nope = queries[:, :, :NOPE].reshape(BLK, NZ, 2, GRP * NOPE)
        rope = queries[:, :, NOPE:].reshape(BLK, NZ, 2, GRP * ROPE)
        q = jnp.concatenate([nope, rope], axis=3).transpose(2, 1, 0, 3)
        q = jnp.broadcast_to(q[None], (NY, 2, NZ, BLK, GRP * (NOPE + ROPE)))
        q = q.reshape(NY * 2 * NZ, BLK, GRP * (NOPE + ROPE))
        q = lax.all_to_all(q, ("y", "core", "z"), split_axis=0, concat_axis=0, tiled=True)
        q = q.reshape(ROWS, GRP * (NOPE + ROPE))

    with jax.named_scope("gate_up_weights"):
        gates = expert_gate[0].reshape(NZ, CHUNK, 128)
        ups = expert_up[0].reshape(NZ, CHUNK, 128)
        downs = expert_down[0]
        gu_out, dn_out = [], []
        for d in range(NZ):
            to = (z + d) % NZ
            g = lax.dynamic_index_in_dim(gates, to, 0, keepdims=False)
            u = lax.dynamic_index_in_dim(ups, to, 0, keepdims=False)
            gu_out.append(jnp.concatenate([g, u], axis=1))
            dn_out.append(lax.dynamic_slice_in_dim(downs, to * CHUNK, CHUNK, axis=1))
        sent = after(gu_out[1:], q)
        gu = [gu_out[0]] + [shift(w, "z", NZ, d + 1) for d, w in enumerate(sent)]

    with jax.named_scope("residual_exchange"):
        score_hi = lax.reduce_precision(route_score, 8, 7)
        score_mid = lax.reduce_precision(route_score - score_hi, 8, 7)
        score_low = route_score - score_hi - score_mid
        info = jnp.concatenate(
            [routes.astype(BF)]
            + [s.astype(BF) for s in (score_hi, score_mid, score_low)]
            + [jnp.zeros((BLK, 128 - 4 * TOP), BF)],
            axis=1,
        )
        rel = []
        for d in range(NZ):
            part = lax.dynamic_slice_in_dim(residual, ((z + d) % NZ) * CHUNK, CHUNK, axis=1)
            part = jnp.concatenate([part, info], axis=1)
            rel.append(shift(part, "z", NZ, d) if d else part)
        owned = absolute(rel, z).reshape(NZ * BLK, CHUNK + 128)
        res = owned[:, :CHUNK].astype(F32)

    with jax.named_scope("routing"):
        tokens = NZ * BLK
        route = owned[:, CHUNK : CHUNK + TOP].astype(jnp.int32)
        score = owned[:, CHUNK + TOP : CHUNK + 4 * TOP].astype(F32).reshape(tokens, 3, TOP)
        score = score[:, 0] + score[:, 1] + score[:, 2]
        weight = 2.5 * score / jnp.sum(score, axis=1, keepdims=True)
        experts = jnp.arange(EXPERTS, dtype=jnp.int32)
        hit = route[:, :, None] == experts
        named = jnp.any(hit, axis=1).astype(jnp.int32).reshape(NZ, BLK, EXPERTS)
        mix = jnp.sum(jnp.where(hit, weight[:, :, None], 0.0), axis=1)
        rank = jnp.cumsum(named, axis=1) - named
        slot = jnp.arange(NZ, dtype=jnp.int32)[:, None, None] * CAP + rank
        slot = jnp.where(named > 0, slot, -1).reshape(tokens, EXPERTS)
        place = slot[:, :, None] == jnp.arange(SLOTS, dtype=jnp.int32)
        pick = place.reshape(tokens, EROWS).astype(BF)
        blend = jnp.where(place, mix[:, :, None], 0.0).reshape(tokens, EROWS)

    with jax.named_scope("attention"):
        doc = lax.dynamic_index_in_dim(response_doc.reshape(NY, NX, NZ, 2, BLK), x, 1, keepdims=False)
        doc = doc.transpose(0, 2, 1, 3).reshape(ROWS)
        ids = jnp.arange(RESP, dtype=jnp.int32).reshape(NY, NX, NZ, 2, BLK)
        ids = lax.dynamic_index_in_dim(ids, x, 1, keepdims=False).transpose(0, 2, 1, 3).reshape(ROWS)
        start = jnp.sum((response_doc[None, :] < doc[:, None]).astype(jnp.int32), axis=1)
        far = jnp.int32(1 << 20)
        first = jnp.where(y == NY - 1, start, -far)[:, None]
        last = jnp.where(y == NY - 1, ids, far)[:, None]
        at = [x * 512]
        for core in (k, 1 - k):
            at += [((x - d) % NX) * 512 + core * HALF for d in range(1, NX)]
        place_of = jnp.stack(at).astype(jnp.int32)
        out = attention(place_of, q, first, last, [latent_cache] + mine + other, absorb_key, absorb_value)

    with jax.named_scope("combine"):
        out = out.reshape(NY, 64, GRP * VDIM + 128)
        out = lax.all_to_all(out, "y", split_axis=0, concat_axis=0, tiled=True)
        stat = out[:, :, GRP * VDIM : GRP * VDIM + 6 * GRP].astype(F32).reshape(NY, 64, 6, GRP)
        top = stat[:, :, 0] + stat[:, :, 1] + stat[:, :, 2]
        total = stat[:, :, 3] + stat[:, :, 4] + stat[:, :, 5]
        scale = LOG2E * (NOPE + ROPE) ** (-0.5)
        share = total * jnp.exp2((top - jnp.max(top, axis=0, keepdims=True)) * scale)
        share = share / jnp.sum(share, axis=0, keepdims=True)
        heads = out[:, :, : GRP * VDIM].astype(F32).reshape(NY, 64, GRP, VDIM)
        head_out = jnp.sum(heads * share[..., None], axis=0).astype(BF).reshape(64, GRP * VDIM)

    with jax.named_scope("out_projection"):
        part = jnp.dot(head_out, out_proj, preferred_element_type=F32).astype(BF)
        part = part.reshape(2, NZ * BLK, NZ, CHUNK).transpose(0, 2, 1, 3).reshape(8, NZ * BLK, CHUNK)
        part = lax.all_to_all(part, ("core", "z"), split_axis=0, concat_axis=0, tiled=True)
        hidden = res + jnp.sum(part.astype(F32), axis=0)

    with jax.named_scope("down_weights"):
        sent = after(dn_out[1:], hidden)
        dn = [dn_out[0]] + [shift(w, "z", NZ, d + 1) for d, w in enumerate(sent)]
        gu = [gu[0]] + list(after(gu[1:], hidden))
        gu_other = [shift(w, "core", 2, 1) for w in gu]

    with jax.named_scope("norm"):
        square = jnp.sum(hidden * hidden, axis=1, keepdims=True)
        square = square + sum(shift(square, "z", NZ, d) for d in range(1, NZ))
        normed = (hidden * lax.rsqrt(square / D + 1e-6) * lax.dynamic_slice_in_dim(norm_gain, z * CHUNK, CHUNK)).astype(BF)

    with jax.named_scope("dispatch"):
        rows = lax.dot_general(pick, normed, (((0,), (0,)), ((), ())), preferred_element_type=F32).astype(BF)
        rows = rows.reshape(EXPERTS, SLOTS, CHUNK)
        rows = lax.all_to_all(rows, ("y", "x"), split_axis=0, concat_axis=0, tiled=True)
        rows = rows.reshape(EROWS, CHUNK)

    with jax.named_scope("experts"):
        dn = [dn[0]] + list(after(dn[1:], rows))
        dn_other = [shift(w, "core", 2, 1) for w in dn]
        gu_pieces = [w for pair in zip(gu, gu_other) for w in pair]
        part = gate_up(z.reshape(1), rows, gu_pieces)
        part = lax.all_to_all(part, "z", split_axis=0, concat_axis=0, tiled=True)
        act = jnp.sum(part.astype(F32), axis=0).reshape(EROWS, 2, 2, 128)
        inner = (jax.nn.silu(act[:, :, 0]) * act[:, :, 1]).astype(BF).reshape(EROWS, 256)
        inners = [inner] + [shift(inner, "z", NZ, d) for d in range(1, NZ)]
        result = down(inners, [w for pair in zip(dn, dn_other) for w in pair])

    with jax.named_scope("return"):
        back = lax.all_to_all(
            result.reshape(EXPERTS, SLOTS, CHUNK), ("y", "x"), split_axis=0, concat_axis=0, tiled=True
        ).reshape(EROWS, CHUNK)
        mixed = jnp.dot(blend, back.astype(F32), precision=lax.Precision.HIGHEST, preferred_element_type=F32)
        done = (hidden + mixed).astype(BF).reshape(NZ, BLK, CHUNK)
        done = lax.all_to_all(done, "z", split_axis=0, concat_axis=0, tiled=True)
        return done.transpose(1, 0, 2).reshape(BLK, D)


def solution(mesh):
    fine = Mesh(mesh.devices.reshape(NY, NX, NZ, 2), ("y", "x", "z", "core"))
    ctx, head = ("y", "x"), ("z", "core")
    both = ctx + head
    in_specs = (
        P(both, None, None),
        P(ctx, None),
        P(head, None, None),
        P(head, None, None),
        P(head, None),
        P(both, None),
        P(),
        P(both, None),
        P(both, None),
        P(),
        P(ctx, None, head),
        P(ctx, None, head),
        P(ctx, head, None),
    )
    return jax.shard_map(shards, mesh=fine, in_specs=in_specs, out_specs=P(both, None), check_vma=False)
```

```python
import functools

import jax
import jax.numpy as jnp
from jax import lax
from jax.experimental import pallas as pl
from jax.experimental.pallas import tpu as pltpu
from jax.sharding import Mesh
from jax.sharding import PartitionSpec as P

D = 7168
NOPE = 128
ROPE = 64
LAT = 512
VDIM = 128
EXPERTS = 16
TOP = 8
RESP = 1024
PROMPT = 7168
NX = 4
NY = 4
NZ = 4
GRP = 8
BLK = 8
CAP = 6
QCOLS = GRP * (NOPE + ROPE) + 128
KEYS = 2048
HALF = 256
ROWS = 256
CHUNK = D // NZ
SLOTS = NZ * CAP
EROWS = 16 * SLOTS
LOG2E = 1.4426950408889634
BF = jnp.bfloat16
F32 = jnp.float32
HIDE = -1e30


def shift(a, axis, n, d):
    return lax.ppermute(a, axis, [(i, (i + d) % n) for i in range(n)])


def split3(v):
    hi = v.astype(BF).astype(F32)
    mid = (v - hi).astype(BF).astype(F32)
    low = (v - hi - mid).astype(BF).astype(F32)
    return hi, mid, low


def cost(flops=0, nbytes=1):
    return pl.CostEstimate(flops=flops, bytes_accessed=nbytes, transcendentals=0)


def call(kernel, name, out_shape, in_specs, scratch, mib=48, **more):
    return pl.pallas_call(
        kernel,
        out_shape=out_shape,
        in_specs=in_specs,
        scratch_shapes=scratch,
        compiler_params=pltpu.CompilerParams(vmem_limit_bytes=mib * 2**20),
        cost_estimate=cost(),
        name=name,
        **more,
    )


VM = pl.BlockSpec(memory_space=pltpu.VMEM)
SM = pl.BlockSpec(memory_space=pltpu.SMEM)
AT = pl.BlockSpec(memory_space=pl.ANY)
PAIR = 2


def attention_kernel(
    pos_ref, q_ref, first_ref, last_ref, c0, c1, c2, c3, s1, s2, s3, ak_ref, av_ref, o_ref, kv, rp, st, hide, sem
):
    g = pl.program_id(0)

    @pl.when(g == 0)
    def _():
        copies = [pltpu.make_async_copy(c0, kv.at[pl.ds(pl.multiple_of(pos_ref[0], HALF), 2 * HALF)], sem.at[0])]
        for i, piece in enumerate((c1, c2, c3, s1, s2, s3)):
            to = kv.at[pl.ds(pl.multiple_of(pos_ref[1 + i], HALF), HALF)]
            copies.append(pltpu.make_async_copy(piece, to, sem.at[1 + i]))
        for c in copies:
            c.start()
        col = lax.broadcasted_iota(jnp.int32, (ROWS, KEYS // 2), 1)
        hide[...] = jnp.where((col >= first_ref[...]) & (col <= last_ref[...]), 0.0, HIDE)
        st[...] = jnp.zeros_like(st)
        for c in copies:
            c.wait()
        r = kv[:, LAT:]
        rp[...] = jnp.concatenate([r, r], axis=1)

    lane = lax.broadcasted_iota(jnp.int32, (ROWS, 128), 1)
    nt = (((1,), (1,)), ((), ()))
    step = 512
    scale = LOG2E * (NOPE + ROPE) ** (-0.5)
    scored = []
    for i in range(PAIR):
        h = g * PAIR + i
        nope = q_ref[:, pl.ds(pl.multiple_of(h * NOPE, NOPE), NOPE)]
        q_lat = jnp.dot(nope, ak_ref[i], preferred_element_type=F32).astype(BF)
        pair = q_ref[:, pl.ds(pl.multiple_of(GRP * NOPE + (h // 2) * 128, 128), 128)].astype(F32)
        rope = jnp.where(lane // ROPE == h % 2, pair, 0.0).astype(BF)
        parts = []
        for j in range(0, KEYS, step):
            s = lax.dot_general(q_lat, kv[j : j + step, :LAT], nt, preferred_element_type=F32)
            s = s + lax.dot_general(rope, rp[j : j + step, :], nt, preferred_element_type=F32)
            if j >= KEYS // 2:
                s = s + hide[:, j - KEYS // 2 : j - KEYS // 2 + step]
            parts.append(s)
        scored.append(parts)
    for i, parts in enumerate(scored):
        h = g * PAIR + i
        top = jnp.max(parts[0], axis=1, keepdims=True)
        for s in parts[1:]:
            top = jnp.maximum(top, jnp.max(s, axis=1, keepdims=True))
        total = jnp.zeros((ROWS, 1), F32)
        acc = jnp.zeros((ROWS, LAT), F32)
        for n, s in enumerate(parts):
            p = jnp.exp2((s - top) * scale)
            total = total + jnp.sum(p, axis=1, keepdims=True)
            acc = acc + jnp.dot(p.astype(BF), kv[n * step : (n + 1) * step, :LAT], preferred_element_type=F32)
        lat = (acc / total).astype(BF)
        o_ref[:, pl.ds(pl.multiple_of(h * VDIM, VDIM), VDIM)] = jnp.dot(
            lat, av_ref[i], preferred_element_type=F32
        ).astype(BF)
        add = jnp.zeros((ROWS, 128), F32)
        for n, v in enumerate(split3(top) + split3(total)):
            add = add + jnp.where(lane == n * GRP + h, v, 0.0)
        st[...] += add

    @pl.when(g == GRP // PAIR - 1)
    def _():
        o_ref[:, GRP * VDIM :] = st[...].astype(BF)


def attention(place, q, first, last, pieces, absorb_key, absorb_value):
    whole = lambda a: pl.BlockSpec(a.shape, lambda g: (0,) * a.ndim)
    return call(
        attention_kernel,
        "attention",
        jax.ShapeDtypeStruct((ROWS, GRP * VDIM + 128), BF),
        [SM, whole(q), whole(first), whole(last)]
        + [AT] * 7
        + [
            pl.BlockSpec((PAIR, NOPE, LAT), lambda g: (g, 0, 0)),
            pl.BlockSpec((PAIR, LAT, VDIM), lambda g: (g, 0, 0)),
        ],
        [
            pltpu.VMEM((KEYS, LAT + ROPE), BF),
            pltpu.VMEM((KEYS, 2 * ROPE), BF),
            pltpu.VMEM((ROWS, 128), F32),
            pltpu.VMEM((ROWS, KEYS // 2), F32),
            pltpu.SemaphoreType.DMA((7,)),
        ],
        grid=(GRP // PAIR,),
        out_specs=pl.BlockSpec((ROWS, GRP * VDIM + 128), lambda g: (0, 0)),
    )(place, q, first, last, *pieces, absorb_key, absorb_value)


def routing_kernel(at_ref, col_ref, q_ref, pick_ref, blend_ref, held, sem):
    rows = q_ref.at[pl.ds(pl.multiple_of(at_ref[0], NZ * BLK), NZ * BLK), pl.ds(QCOLS - 128, 128)]
    copy = pltpu.make_async_copy(rows, held, sem)
    copy.start()
    copy.wait()
    info = held[...].astype(F32)
    rows = NZ * BLK
    route = info[:, :TOP]
    score = info[:, TOP : 2 * TOP] + info[:, 2 * TOP : 3 * TOP] + info[:, 3 * TOP : 4 * TOP]
    weight = 2.5 * score / jnp.sum(score, axis=1, keepdims=True)
    expert, block, slot = col_ref[0:1, :], col_ref[1:2, :], col_ref[2:3, :]
    named = jnp.zeros((rows, EROWS), F32)
    mix = jnp.zeros((rows, EROWS), F32)
    for n in range(TOP):
        hit = route[:, n : n + 1] == expert
        named = named + jnp.where(hit, 1.0, 0.0)
        mix = mix + jnp.where(hit, weight[:, n : n + 1], 0.0)
    i = lax.broadcasted_iota(jnp.int32, (rows, rows), 0)
    j = lax.broadcasted_iota(jnp.int32, (rows, rows), 1)
    ahead = jnp.where((j < i) & (j // BLK == i // BLK), 1.0, 0.0).astype(BF)
    rank = jnp.dot(ahead, named.astype(BF), preferred_element_type=F32)
    mine = (lax.broadcasted_iota(jnp.int32, (rows, EROWS), 0) // BLK).astype(F32)
    place = (named > 0.5) & (block == mine) & (slot == rank)
    pick_ref[...] = jnp.where(place, 1.0, 0.0).astype(BF)
    blend_ref[...] = jnp.where(place, mix, 0.0)


def routing(at, q):
    col = jnp.arange(EROWS, dtype=jnp.int32)
    cols = jnp.stack([col // SLOTS, col % SLOTS // CAP, col % CAP] + [col * 0] * 5).astype(F32)
    rows = NZ * BLK
    return call(
        routing_kernel,
        "routing",
        (jax.ShapeDtypeStruct((rows, EROWS), BF), jax.ShapeDtypeStruct((rows, EROWS), F32)),
        [SM, VM, AT],
        [pltpu.VMEM((rows, 128), BF), pltpu.SemaphoreType.DMA],
        out_specs=(VM, VM),
    )(at, cols, q)


def project_kernel(own_ref, o_ref, w_ref, res_ref, out_ref, head_out):
    @pl.when(pl.program_id(0) == 0)
    def _():
        tops, totals = [], []
        for s in range(NY):
            st = o_ref[s, :, GRP * VDIM :].astype(F32)
            part = [st[:, n * GRP : (n + 1) * GRP] for n in range(6)]
            tops.append(part[0] + part[1] + part[2])
            totals.append(part[3] + part[4] + part[5])
        top = jnp.maximum(jnp.maximum(tops[0], tops[1]), jnp.maximum(tops[2], tops[3]))
        scale = LOG2E * (NOPE + ROPE) ** (-0.5)
        share = [t * jnp.exp2((m - top) * scale) for m, t in zip(tops, totals)]
        whole = share[0] + share[1] + share[2] + share[3]
        share = [s / whole for s in share]
        for h in range(GRP):
            at = slice(h * VDIM, (h + 1) * VDIM)
            total = sum(o_ref[s, :, at].astype(F32) * share[s][:, h : h + 1] for s in range(NY))
            head_out[:, at] = total.astype(BF)

    part = jnp.dot(head_out[...], w_ref[...], preferred_element_type=F32)
    row = lax.broadcasted_iota(jnp.int32, part.shape, 0) // BLK
    res = jnp.concatenate([res_ref[...].astype(F32)] * 8, axis=0)
    part = (part + jnp.where(row == own_ref[0], res, 0.0)).astype(BF)
    out_ref[0, 0] = part[: NZ * BLK]
    out_ref[1, 0] = part[NZ * BLK :]


def project(own, o, out_proj, residual):
    width = CHUNK // 2
    return call(
        project_kernel,
        "project",
        jax.ShapeDtypeStruct((2, NZ, NZ * BLK, CHUNK), BF),
        [
            SM,
            pl.BlockSpec(o.shape, lambda j: (0, 0, 0)),
            pl.BlockSpec((GRP * VDIM, width), lambda j: (0, j)),
            pl.BlockSpec((BLK, width), lambda j: (0, j)),
        ],
        [pltpu.VMEM((64, GRP * VDIM), BF)],
        grid=(D // width,),
        out_specs=pl.BlockSpec((2, 1, NZ * BLK, width), lambda j: (0, j // 2, 0, j % 2)),
    )(own, o, out_proj, residual)


def spread_kernel(part_ref, gain_ref, pick_ref, hidden_ref, rows_ref):
    hidden = part_ref[0].astype(F32)
    for s in range(1, 8):
        hidden = hidden + part_ref[s].astype(F32)
    hidden_ref[...] = hidden
    scaled = (hidden * gain_ref[...]).astype(BF)
    tn = (((0,), (0,)), ((), ()))
    rows_ref[...] = lax.dot_general(pick_ref[...], scaled, tn, preferred_element_type=F32).astype(BF)


def spread(part, gain, pick):
    return call(
        spread_kernel,
        "spread",
        (jax.ShapeDtypeStruct((NZ * BLK, CHUNK), F32), jax.ShapeDtypeStruct((EROWS, CHUNK), BF)),
        [VM] * 3,
        [],
        out_specs=(VM, VM),
    )(part, gain, pick)


def gate_up_kernel(z_ref, x_ref, gain_ref, *refs):
    pieces, (o_ref, square_ref, w, sem) = refs[:8], refs[8:]
    copies = [
        pltpu.make_async_copy(p, w.at[:, pl.ds(i * 256, 256)], sem.at[i]) for i, p in enumerate(pieces)
    ]
    for c in copies:
        c.start()
    x = x_ref[...]
    raw = x.astype(F32) * gain_ref[...]
    ones = jnp.ones((8, CHUNK), BF)
    square_ref[...] = lax.dot_general(
        ones, (raw * raw).astype(BF), (((1,), (1,)), ((), ())), preferred_element_type=F32
    )
    for d in range(NZ):
        copies[2 * d].wait()
        copies[2 * d + 1].wait()
        part = jnp.dot(x, w[:, d * 512 : (d + 1) * 512], preferred_element_type=F32).astype(BF)
        o_ref[lax.rem(z_ref[0] + NZ - d, NZ)] = part


def gate_up(z, x, gain, pieces):
    return call(
        gate_up_kernel,
        "gate_up",
        (jax.ShapeDtypeStruct((NZ, EROWS, 512), BF), jax.ShapeDtypeStruct((8, EROWS), F32)),
        [SM, VM, VM] + [AT] * 8,
        [pltpu.VMEM((CHUNK, 2048), BF), pltpu.SemaphoreType.DMA((8,))],
        out_specs=(VM, VM),
    )(z, x, gain, *pieces)


def inner_kernel(part_ref, s0, s1, s2, s3, out_ref):
    square = s0[...] + s1[...] + s2[...] + s3[...]
    scale = lax.rsqrt(square / D + 1e-6).T[:, :1]
    total = part_ref[0].astype(F32)
    for s in range(1, NZ):
        total = total + part_ref[s].astype(F32)
    total = total * scale
    for k in range(2):
        gate, up = total[:, k * 256 : k * 256 + 128], total[:, k * 256 + 128 : k * 256 + 256]
        out_ref[:, k * 128 : (k + 1) * 128] = (gate / (1.0 + jnp.exp(-gate)) * up).astype(BF)


def inner_act(part, squares):
    return call(
        inner_kernel, "inner_act", jax.ShapeDtypeStruct((EROWS, 256), BF), [VM] * 5, [], out_specs=VM
    )(part, *squares)


def down_kernel(i0, i1, i2, i3, *refs):
    pieces, (o_ref, w, sem) = refs[:8], refs[8:]
    copies = [
        pltpu.make_async_copy(p, w.at[pl.ds(i * 128, 128)], sem.at[i]) for i, p in enumerate(pieces)
    ]
    for c in copies:
        c.start()
    inner = jnp.concatenate([i0[...], i1[...], i2[...], i3[...]], axis=1)
    for c in copies:
        c.wait()
    o_ref[...] = jnp.dot(inner, w[...], preferred_element_type=F32).astype(BF)


def down(inners, pieces):
    return call(
        down_kernel,
        "down",
        jax.ShapeDtypeStruct((EROWS, CHUNK), BF),
        [VM] * 4 + [AT] * 8,
        [pltpu.VMEM((1024, CHUNK), BF), pltpu.SemaphoreType.DMA((8,))],
        out_specs=VM,
    )(*inners, *pieces)


def after(arrays, token):
    out = lax.optimization_barrier(tuple(arrays) + (token,))
    return out[:-1]


def shards(
    queries,
    latent_cache,
    absorb_key,
    absorb_value,
    out_proj,
    residual,
    norm_gain,
    routes,
    route_score,
    response_doc,
    expert_gate,
    expert_up,
    expert_down,
):
    x, y, z, k = (lax.axis_index(a) for a in ("x", "y", "z", "core"))

    with jax.named_scope("cache_gather"):
        half = lax.dynamic_slice_in_dim(latent_cache, k * HALF, HALF, axis=0)
        mine = [shift(half, "x", NX, d) for d in range(1, NX)]

    with jax.named_scope("query_exchange"):
        score_hi = lax.reduce_precision(route_score, 8, 7)
        score_mid = lax.reduce_precision(route_score - score_hi, 8, 7)
        score_low = route_score - score_hi - score_mid
        info = jnp.concatenate(
            [routes.astype(BF)]
            + [s.astype(BF) for s in (score_hi, score_mid, score_low)]
            + [jnp.zeros((BLK, 128 - 4 * TOP), BF)],
            axis=1,
        )
        info = jnp.broadcast_to(info[:, None, None], (BLK, NZ, 2, 128))
        nope = queries[:, :, :NOPE].reshape(BLK, NZ, 2, GRP * NOPE)
        rope = queries[:, :, NOPE:].reshape(BLK, NZ, 2, GRP * ROPE)
        q = jnp.concatenate([nope, rope, info], axis=3).transpose(2, 1, 0, 3)
        q = jnp.broadcast_to(q[None], (NY, 2, NZ, BLK, QCOLS))
        q = q.reshape(NY * 2 * NZ, BLK, QCOLS)
        (q,) = after([q], mine[0])
        q = lax.all_to_all(q, ("y", "core", "z"), split_axis=0, concat_axis=0, tiled=True)
        q = q.reshape(ROWS, QCOLS)

    with jax.named_scope("weights"):
        gates = expert_gate[0].reshape(NZ, CHUNK, 128)
        ups = expert_up[0].reshape(NZ, CHUNK, 128)
        downs = expert_down[0]
        gu, dn = [], []
        for d in range(NZ):
            to = (z + d) % NZ
            g = lax.dynamic_index_in_dim(gates, to, 0, keepdims=False)
            u = lax.dynamic_index_in_dim(ups, to, 0, keepdims=False)
            gu.append(jnp.concatenate([g, u], axis=1))
            dn.append(lax.dynamic_slice_in_dim(downs, to * CHUNK, CHUNK, axis=1))
        gu[1], gu[3] = shift(gu[1], "z", NZ, 1), shift(gu[3], "z", NZ, 3)

    with jax.named_scope("cache_share"):
        other = [shift(m, "core", 2, 1) for m in mine]

    with jax.named_scope("attention"):
        doc = lax.dynamic_index_in_dim(response_doc.reshape(NY, NX, NZ, 2, BLK), x, 1, keepdims=False)
        doc = doc.transpose(0, 2, 1, 3).reshape(ROWS)
        ids = jnp.arange(RESP, dtype=jnp.int32).reshape(NY, NX, NZ, 2, BLK)
        ids = lax.dynamic_index_in_dim(ids, x, 1, keepdims=False).transpose(0, 2, 1, 3).reshape(ROWS)
        start = jnp.sum((response_doc[None, :] < doc[:, None]).astype(jnp.int32), axis=1)
        far = jnp.int32(1 << 20)
        first = jnp.where(y == NY - 1, start, -far)[:, None]
        last = jnp.where(y == NY - 1, ids, far)[:, None]
        at = [x * 512]
        for core in (k, 1 - k):
            at += [((x - d) % NX) * 512 + core * HALF for d in range(1, NX)]
        place_of = jnp.stack(at).astype(jnp.int32)

        q, gu[1], gu[3] = lax.optimization_barrier((q, gu[1], gu[3]))
        ahead = after([gu[2], dn[1], dn[3]], q)
        gu[2], dn[1], dn[3] = shift(ahead[0], "z", NZ, 2), shift(ahead[1], "z", NZ, 1), shift(ahead[2], "z", NZ, 3)
        out = attention(place_of, q, first, last, [latent_cache] + mine + other, absorb_key, absorb_value)

    with jax.named_scope("combine"):
        out = lax.all_to_all(out.reshape(NY, 64, -1), "y", split_axis=0, concat_axis=0, tiled=True)

    with jax.named_scope("routing"):
        pick, blend = routing(((y * 2 + k) * NZ * BLK).reshape(1), after([q], out)[0])

    with jax.named_scope("out_projection"):
        out, gu[2], dn[1], dn[3] = lax.optimization_barrier((out, gu[2], dn[1], dn[3]))
        gu_other = [shift(w, "core", 2, 1) for w in after(gu, out)]
        part = project((k * NZ + z).reshape(1), out, out_proj, residual)
        part = part.reshape(8, NZ * BLK, CHUNK)
        part = lax.all_to_all(part, ("core", "z"), split_axis=0, concat_axis=0, tiled=True)

    with jax.named_scope("dispatch"):
        gain = lax.dynamic_slice_in_dim(norm_gain, z * CHUNK, CHUNK)[None]
        part, *gu_other = lax.optimization_barrier((part, *gu_other))
        (ahead,) = after([dn[2]], part)
        dn[2] = shift(ahead, "z", NZ, 2)
        hidden, rows = spread(part, gain, pick)
        rows = rows.reshape(EXPERTS, SLOTS, CHUNK)
        rows = lax.all_to_all(rows, ("y", "x"), split_axis=0, concat_axis=0, tiled=True)
        rows = rows.reshape(EROWS, CHUNK)

    with jax.named_scope("experts"):
        rows, dn[2] = lax.optimization_barrier((rows, dn[2]))
        dn_other = [shift(w, "core", 2, 1) for w in after(dn, rows)]
        part, square = gate_up(z.reshape(1), rows, 1.0 / gain, [w for pair in zip(gu, gu_other) for w in pair])
        squares = [square] + [shift(square, "z", NZ, d) for d in range(1, NZ)]
        part, *dn_other = lax.optimization_barrier((part, *dn_other))
        part = lax.all_to_all(part, "z", split_axis=0, concat_axis=0, tiled=True)
        inner = inner_act(part, squares)
        inners = [inner] + [shift(inner, "z", NZ, d) for d in range(1, NZ)]
        result = down(inners, [w for pair in zip(dn, dn_other) for w in pair])

    with jax.named_scope("return"):
        back = lax.all_to_all(
            result.reshape(EXPERTS, SLOTS, CHUNK), ("y", "x"), split_axis=0, concat_axis=0, tiled=True
        ).reshape(EROWS, CHUNK)
        mixed = jnp.dot(blend, back.astype(F32), precision=lax.Precision.HIGHEST, preferred_element_type=F32)
        done = (hidden + mixed).astype(BF).reshape(NZ, BLK, CHUNK)
        done = lax.all_to_all(done, "z", split_axis=0, concat_axis=0, tiled=True)
        return done.transpose(1, 0, 2).reshape(BLK, D)


def solution(mesh):
    fine = Mesh(mesh.devices.reshape(NY, NX, NZ, 2), ("y", "x", "z", "core"))
    ctx, head = ("y", "x"), ("z", "core")
    both = ctx + head
    in_specs = (
        P(both, None, None),
        P(ctx, None),
        P(head, None, None),
        P(head, None, None),
        P(head, None),
        P(both, None),
        P(),
        P(both, None),
        P(both, None),
        P(),
        P(ctx, None, head),
        P(ctx, None, head),
        P(ctx, head, None),
    )
    return jax.shard_map(shards, mesh=fine, in_specs=in_specs, out_specs=P(both, None), check_vma=False)
```

```python
import functools

import jax
import jax.numpy as jnp
from jax import lax
from jax.experimental import pallas as pl
from jax.experimental.pallas import tpu as pltpu
from jax.sharding import Mesh
from jax.sharding import PartitionSpec as P

D = 7168
NOPE = 128
ROPE = 64
LAT = 512
VDIM = 128
EXPERTS = 16
TOP = 8
RESP = 1024
PROMPT = 7168
NX = 4
NY = 4
NZ = 4
GRP = 8
BLK = 8
CAP = 6
QCOLS = GRP * (NOPE + ROPE) + 128
KEYS = 2048
HALF = 256
ROWS = 256
CHUNK = D // NZ
SLOTS = NZ * CAP
EROWS = 16 * SLOTS
LOG2E = 1.4426950408889634
BF = jnp.bfloat16
F32 = jnp.float32
HIDE = -1e30


def shift(a, axis, n, d):
    return lax.ppermute(a, axis, [(i, (i + d) % n) for i in range(n)])


def split3(v):
    hi = v.astype(BF).astype(F32)
    mid = (v - hi).astype(BF).astype(F32)
    low = (v - hi - mid).astype(BF).astype(F32)
    return hi, mid, low


def cost(flops=0, nbytes=1):
    return pl.CostEstimate(flops=flops, bytes_accessed=nbytes, transcendentals=0)


def call(kernel, name, out_shape, in_specs, scratch, mib=32, **more):
    return pl.pallas_call(
        kernel,
        out_shape=out_shape,
        in_specs=in_specs,
        scratch_shapes=scratch,
        compiler_params=pltpu.CompilerParams(vmem_limit_bytes=mib * 2**20),
        cost_estimate=cost(),
        name=name,
        **more,
    )


VM = pl.BlockSpec(memory_space=pltpu.VMEM)
SM = pl.BlockSpec(memory_space=pltpu.SMEM)
AT = pl.BlockSpec(memory_space=pltpu.HBM)
PAIR = 2


def attention_kernel(
    pos_ref, q_ref, first_ref, last_ref, c0, c1, c2, c3, s1, s2, s3, ak_ref, av_ref, o0, o1, o2, o3, kv, rp, st, hide, sem
):
    g = pl.program_id(0)
    outs = (o0, o1, o2, o3)

    def query(at):
        blocks = [lax.rem(pos_ref[7] + d, NY) for d in range(NY)]
        return jnp.concatenate([q_ref[b, :, pl.ds(pl.multiple_of(at, 128), 128)] for b in blocks], axis=0)

    @pl.when(g == 0)
    def _():
        copies = [pltpu.make_async_copy(c0, kv.at[pl.ds(pl.multiple_of(pos_ref[0], HALF), 2 * HALF)], sem.at[0])]
        for i, piece in enumerate((c1, c2, c3, s1, s2, s3)):
            to = kv.at[pl.ds(pl.multiple_of(pos_ref[1 + i], HALF), HALF)]
            copies.append(pltpu.make_async_copy(piece, to, sem.at[1 + i]))
        for c in copies:
            c.start()
        col = lax.broadcasted_iota(jnp.int32, (ROWS, KEYS // 2), 1)
        hide[...] = jnp.where((col >= first_ref[...]) & (col <= last_ref[...]), 0.0, HIDE)
        st[...] = jnp.zeros_like(st)
        for c in copies:
            c.wait()
        r = kv[:, LAT:]
        rp[...] = jnp.concatenate([r, r], axis=1)

    lane = lax.broadcasted_iota(jnp.int32, (ROWS, 128), 1)
    nt = (((1,), (1,)), ((), ()))
    step = 512
    scale = LOG2E * (NOPE + ROPE) ** (-0.5)
    scored = []
    for i in range(PAIR):
        h = g * PAIR + i
        nope = query(h * NOPE)
        q_lat = jnp.dot(nope, ak_ref[i], preferred_element_type=F32).astype(BF)
        pair = query(GRP * NOPE + (h // 2) * 128).astype(F32)
        rope = jnp.where(lane // ROPE == h % 2, pair, 0.0).astype(BF)
        parts = []
        for j in range(0, KEYS, step):
            s = lax.dot_general(q_lat, kv[j : j + step, :LAT], nt, preferred_element_type=F32)
            s = s + lax.dot_general(rope, rp[j : j + step, :], nt, preferred_element_type=F32)
            if j >= KEYS // 2:
                s = s + hide[:, j - KEYS // 2 : j - KEYS // 2 + step]
            parts.append(s)
        scored.append(parts)
    for i, parts in enumerate(scored):
        h = g * PAIR + i
        top = jnp.max(parts[0], axis=1, keepdims=True)
        for s in parts[1:]:
            top = jnp.maximum(top, jnp.max(s, axis=1, keepdims=True))
        total = jnp.zeros((ROWS, 1), F32)
        acc = jnp.zeros((ROWS, LAT), F32)
        for n, s in enumerate(parts):
            p = jnp.exp2((s - top) * scale)
            total = total + jnp.sum(p, axis=1, keepdims=True)
            acc = acc + jnp.dot(p.astype(BF), kv[n * step : (n + 1) * step, :LAT], preferred_element_type=F32)
        lat = (acc / total).astype(BF)
        head = jnp.dot(lat, av_ref[i], preferred_element_type=F32).astype(BF)
        for d, o in enumerate(outs):
            o[:, pl.ds(pl.multiple_of(h * VDIM, VDIM), VDIM)] = head[d * 64 : (d + 1) * 64]
        add = jnp.zeros((ROWS, 128), F32)
        for n, v in enumerate(split3(top) + split3(total)):
            add = add + jnp.where(lane == n * GRP + h, v, 0.0)
        st[...] += add

    @pl.when(g == GRP // PAIR - 1)
    def _():
        for d, o in enumerate(outs):
            o[:, GRP * VDIM :] = st[d * 64 : (d + 1) * 64, :].astype(BF)


def attention(place, q, first, last, pieces, absorb_key, absorb_value):
    whole = lambda a: pl.BlockSpec(a.shape, lambda g: (0,) * a.ndim)
    return call(
        attention_kernel,
        "attention",
        (jax.ShapeDtypeStruct((64, GRP * VDIM + 128), BF),) * NY,
        [SM, whole(q), whole(first), whole(last)]
        + [AT] * 7
        + [
            pl.BlockSpec((PAIR, NOPE, LAT), lambda g: (g, 0, 0)),
            pl.BlockSpec((PAIR, LAT, VDIM), lambda g: (g, 0, 0)),
        ],
        [
            pltpu.VMEM((KEYS, LAT + ROPE), BF),
            pltpu.VMEM((KEYS, 2 * ROPE), BF),
            pltpu.VMEM((ROWS, 128), F32),
            pltpu.VMEM((ROWS, KEYS // 2), F32),
            pltpu.SemaphoreType.DMA((7,)),
        ],
        grid=(GRP // PAIR,),
        out_specs=(pl.BlockSpec((64, GRP * VDIM + 128), lambda g: (0, 0)),) * NY,
    )(place, q, first, last, *pieces, absorb_key, absorb_value)


def routing_kernel(at_ref, col_ref, q_ref, pick_ref, blend_ref, held, sem):
    rows = q_ref.at[pl.ds(pl.multiple_of(at_ref[0], NZ * BLK), NZ * BLK), pl.ds(QCOLS - 128, 128)]
    copy = pltpu.make_async_copy(rows, held, sem)
    copy.start()
    copy.wait()
    info = held[...].astype(F32)
    rows = NZ * BLK
    route = info[:, :TOP]
    score = info[:, TOP : 2 * TOP] + info[:, 2 * TOP : 3 * TOP] + info[:, 3 * TOP : 4 * TOP]
    weight = 2.5 * score / jnp.sum(score, axis=1, keepdims=True)
    expert, block, slot = col_ref[0:1, :], col_ref[1:2, :], col_ref[2:3, :]
    named = jnp.zeros((rows, EROWS), F32)
    mix = jnp.zeros((rows, EROWS), F32)
    for n in range(TOP):
        hit = route[:, n : n + 1] == expert
        named = named + jnp.where(hit, 1.0, 0.0)
        mix = mix + jnp.where(hit, weight[:, n : n + 1], 0.0)
    i = lax.broadcasted_iota(jnp.int32, (rows, rows), 0)
    j = lax.broadcasted_iota(jnp.int32, (rows, rows), 1)
    ahead = jnp.where((j < i) & (j // BLK == i // BLK), 1.0, 0.0).astype(BF)
    rank = jnp.dot(ahead, named.astype(BF), preferred_element_type=F32)
    mine = (lax.broadcasted_iota(jnp.int32, (rows, EROWS), 0) // BLK).astype(F32)
    place = (named > 0.5) & (block == mine) & (slot == rank)
    pick_ref[...] = jnp.where(place, 1.0, 0.0).astype(BF)
    blend_ref[...] = jnp.where(place, mix, 0.0)


def routing(at, q):
    col = jnp.arange(EROWS, dtype=jnp.int32)
    cols = jnp.stack([col // SLOTS, col % SLOTS // CAP, col % CAP] + [col * 0] * 5).astype(F32)
    rows = NZ * BLK
    return call(
        routing_kernel,
        "routing",
        (jax.ShapeDtypeStruct((rows, EROWS), BF), jax.ShapeDtypeStruct((rows, EROWS), F32)),
        [SM, VM, AT],
        [pltpu.VMEM((rows, 128), BF), pltpu.SemaphoreType.DMA],
        out_specs=(VM, VM),
    )(at, cols, q)


def merge_kernel(o0, o1, o2, o3, head_out):
    outs = (o0, o1, o2, o3)
    tops, totals = [], []
    for o in outs:
        st = o[:, GRP * VDIM :].astype(F32)
        part = [st[:, n * GRP : (n + 1) * GRP] for n in range(6)]
        tops.append(part[0] + part[1] + part[2])
        totals.append(part[3] + part[4] + part[5])
    top = jnp.maximum(jnp.maximum(tops[0], tops[1]), jnp.maximum(tops[2], tops[3]))
    scale = LOG2E * (NOPE + ROPE) ** (-0.5)
    share = [t * jnp.exp2((m - top) * scale) for m, t in zip(tops, totals)]
    whole = share[0] + share[1] + share[2] + share[3]
    share = [s / whole for s in share]
    for h in range(GRP):
        at = slice(h * VDIM, (h + 1) * VDIM)
        total = sum(o[:, at].astype(F32) * share[s][:, h : h + 1] for s, o in enumerate(outs))
        head_out[:, at] = total.astype(BF)


def merge(outs):
    return call(
        merge_kernel,
        "merge",
        jax.ShapeDtypeStruct((64, GRP * VDIM), BF),
        [VM] * 4,
        [],
        out_specs=VM,
    )(*outs)


def stage_kernel(token_ref, w_ref, held_ref, sem):
    rows = w_ref.shape[0] // 8
    copies = [
        pltpu.make_async_copy(w_ref.at[pl.ds(i * rows, rows)], held_ref.at[pl.ds(i * rows, rows)], sem.at[i])
        for i in range(8)
    ]
    for c in copies:
        c.start()
    for c in copies:
        c.wait()


def stage(token, w):
    return call(
        stage_kernel,
        "stage",
        pltpu.VMEM(w.shape, w.dtype),
        [AT, AT],
        [pltpu.SemaphoreType.DMA((8,))],
        mib=44,
        out_specs=VM,
    )(token, w)


def project_kernel(ways, own_ref, head_ref, w_ref, res_ref, *outs):
    half = NZ * BLK
    for n, d in enumerate(ways):
        keep_ref, send_ref = outs[2 * n], outs[2 * n + 1]
        at = pl.ds(pl.multiple_of(lax.rem(own_ref[1] + d, NZ) * CHUNK, CHUNK), CHUNK)
        part = jnp.dot(head_ref[...], w_ref[:, at], preferred_element_type=F32)
        row = lax.broadcasted_iota(jnp.int32, part.shape, 0) // BLK
        res = jnp.concatenate([res_ref[:, at].astype(F32)] * 8, axis=0)
        part = part + jnp.where(row == own_ref[0] * NZ + own_ref[1], res, 0.0)
        low = jnp.broadcast_to(own_ref[0], (half, CHUNK)) == 0
        keep_ref[...] = jnp.where(low, part[:half], part[half:])
        send_ref[...] = jnp.where(low, part[half:], part[:half]).astype(BF)


def project(ways, own, head_out, out_proj, residual):
    shape = (NZ * BLK, CHUNK)
    return call(
        functools.partial(project_kernel, ways),
        "project",
        (jax.ShapeDtypeStruct(shape, F32), jax.ShapeDtypeStruct(shape, BF)) * len(ways),
        [SM] + [VM] * 3,
        [],
        out_specs=(VM,) * (2 * len(ways)),
    )(own, head_out, out_proj, residual)


def fold_kernel(n, *refs):
    for keep, got, out in zip(refs[:n], refs[n : 2 * n], refs[2 * n :]):
        out[...] = (keep[...] + got[...].astype(F32)).astype(BF)


def fold(keeps, gots):
    n = len(keeps)
    return call(
        functools.partial(fold_kernel, n),
        "fold",
        (jax.ShapeDtypeStruct((NZ * BLK, CHUNK), BF),) * n,
        [VM] * (2 * n),
        [],
        out_specs=(VM,) * n,
    )(*keeps, *gots)


def spread_kernel(keep_ref, got_ref, p1, p2, p3, gain_ref, pick_ref, hidden_ref, rows_ref):
    hidden = keep_ref[...] + got_ref[...].astype(F32) + p1[...].astype(F32) + p2[...].astype(F32) + p3[...].astype(F32)
    hidden_ref[...] = hidden
    scaled = (hidden * gain_ref[...]).astype(BF)
    tn = (((0,), (0,)), ((), ()))
    rows_ref[...] = lax.dot_general(pick_ref[...], scaled, tn, preferred_element_type=F32).astype(BF)


def spread(parts, gain, pick):
    return call(
        spread_kernel,
        "spread",
        (jax.ShapeDtypeStruct((NZ * BLK, CHUNK), F32), pltpu.VMEM((EROWS, CHUNK), BF)),
        [VM] * 7,
        [],
        out_specs=(VM, VM),
    )(*parts, gain, pick)


def gate_up_kernel(z_ref, x_ref, gain_ref, *refs):
    pieces, (o_ref, w, sem) = refs[:8], refs[8:]
    copies = [
        pltpu.make_async_copy(p, w.at[:, pl.ds(i * 256, 256)], sem.at[i]) for i, p in enumerate(pieces)
    ]
    for c in copies:
        c.start()
    x = x_ref[...]
    raw = x.astype(F32) * gain_ref[...]
    ones = jnp.ones((8, CHUNK), BF)
    square = lax.dot_general(
        ones, (raw * raw).astype(BF), (((1,), (1,)), ((), ())), preferred_element_type=F32
    )
    row = lax.broadcasted_iota(jnp.int32, square.shape, 0)
    hi, mid, low = split3(square)
    coded = jnp.where(row == 0, hi, jnp.where(row == 1, mid, jnp.where(row == 2, low, 0.0)))
    coded = jnp.concatenate([coded, jnp.zeros_like(coded)], axis=0).astype(BF)
    coded = jnp.concatenate([coded, jnp.zeros((16, 512 - EROWS), BF)], axis=1)
    for d in range(NZ):
        copies[2 * d].wait()
        copies[2 * d + 1].wait()
        part = jnp.dot(x, w[:, d * 512 : (d + 1) * 512], preferred_element_type=F32).astype(BF)
        to = lax.rem(z_ref[0] + NZ - d, NZ)
        o_ref[to, :EROWS] = part
        o_ref[to, EROWS:] = coded


def gate_up(z, x, gain, pieces):
    return call(
        gate_up_kernel,
        "gate_up",
        pltpu.VMEM((NZ, EROWS + 16, 512), BF),
        [SM, VM, VM] + [AT] * 8,
        [pltpu.VMEM((CHUNK, 2048), BF), pltpu.SemaphoreType.DMA((8,))],
        out_specs=VM,
    )(z, x, gain, *pieces)


def inner_kernel(part_ref, out_ref):
    total = part_ref[0].astype(F32)
    for s in range(1, NZ):
        total = total + part_ref[s].astype(F32)
    square = jnp.sum(total[EROWS : EROWS + 8], axis=0, keepdims=True)
    scale = lax.rsqrt(jnp.broadcast_to(square[:, :EROWS], (8, EROWS)) / D + 1e-6).T[:, :1]
    total = total[:EROWS] * scale
    for k in range(2):
        gate, up = total[:, k * 256 : k * 256 + 128], total[:, k * 256 + 128 : k * 256 + 256]
        out_ref[:, k * 128 : (k + 1) * 128] = (gate / (1.0 + jnp.exp(-gate)) * up).astype(BF)


def inner_act(part):
    return call(inner_kernel, "inner_act", jax.ShapeDtypeStruct((EROWS, 256), BF), [VM], [], out_specs=VM)(part)


def down_kernel(i0, i1, i2, i3, *refs):
    pieces, (o_ref, w, sem) = refs[:8], refs[8:]
    copies = [
        pltpu.make_async_copy(p, w.at[pl.ds(i * 128, 128)], sem.at[i]) for i, p in enumerate(pieces)
    ]
    for c in copies:
        c.start()
    inner = jnp.concatenate([i0[...], i1[...], i2[...], i3[...]], axis=1)
    for c in copies:
        c.wait()
    o_ref[...] = jnp.dot(inner, w[...], preferred_element_type=F32).astype(BF)


def down(inners, pieces):
    return call(
        down_kernel,
        "down",
        pltpu.VMEM((EROWS, CHUNK), BF),
        [VM] * 4 + [AT] * 8,
        [pltpu.VMEM((1024, CHUNK), BF), pltpu.SemaphoreType.DMA((8,))],
        out_specs=VM,
    )(*inners, *pieces)


def after(arrays, token):
    out = lax.optimization_barrier(tuple(arrays) + (token,))
    return out[:-1]


def turned(a, by):
    return lax.dynamic_slice_in_dim(jnp.concatenate([a, a]), by, a.shape[0], axis=0).reshape(-1)


def shards(
    queries,
    latent_cache,
    absorb_key,
    absorb_value,
    out_proj,
    residual,
    norm_gain,
    routes,
    route_score,
    response_doc,
    expert_gate,
    expert_up,
    expert_down,
):
    x, y, z, k = (lax.axis_index(a) for a in ("x", "y", "z", "core"))

    with jax.named_scope("cache_gather"):
        half = lax.dynamic_slice_in_dim(latent_cache, k * HALF, HALF, axis=0)
        mine = [shift(half, "x", NX, d) for d in range(1, NX)]

    with jax.named_scope("query_exchange"):
        score_hi = lax.reduce_precision(route_score, 8, 7)
        score_mid = lax.reduce_precision(route_score - score_hi, 8, 7)
        score_low = route_score - score_hi - score_mid
        info = jnp.concatenate(
            [routes.astype(BF)]
            + [s.astype(BF) for s in (score_hi, score_mid, score_low)]
            + [jnp.zeros((BLK, 128 - 4 * TOP), BF)],
            axis=1,
        )
        info = jnp.broadcast_to(info[:, None, None], (BLK, NZ, 2, 128))
        nope = queries[:, :, :NOPE].reshape(BLK, NZ, 2, GRP * NOPE)
        rope = queries[:, :, NOPE:].reshape(BLK, NZ, 2, GRP * ROPE)
        q = jnp.concatenate([nope, rope, info], axis=3).transpose(2, 1, 0, 3)
        q = jnp.broadcast_to(q[None], (NY, 2, NZ, BLK, QCOLS))
        q = q.reshape(NY * 2 * NZ, BLK, QCOLS)
        (q,) = after([q], mine[0])
        q = lax.all_to_all(q, ("y", "core", "z"), split_axis=0, concat_axis=0, tiled=True)
        q = q.reshape(ROWS, QCOLS)

    with jax.named_scope("weights"):
        gates = expert_gate[0].reshape(NZ, CHUNK, 128)
        ups = expert_up[0].reshape(NZ, CHUNK, 128)
        downs = expert_down[0]
        gu, dn = [], []
        for d in range(NZ):
            to = (z + d) % NZ
            g = lax.dynamic_index_in_dim(gates, to, 0, keepdims=False)
            u = lax.dynamic_index_in_dim(ups, to, 0, keepdims=False)
            gu.append(jnp.concatenate([g, u], axis=1))
            dn.append(lax.dynamic_slice_in_dim(downs, to * CHUNK, CHUNK, axis=1))
    with jax.named_scope("cache_share"):
        other = [shift(m, "core", 2, 1) for m in mine]

    with jax.named_scope("attention"):
        doc = lax.dynamic_index_in_dim(response_doc.reshape(NY, NX, NZ, 2, BLK), x, 1, keepdims=False)
        doc = turned(doc.transpose(0, 2, 1, 3).reshape(NY, 64), y)
        ids = jnp.arange(RESP, dtype=jnp.int32).reshape(NY, NX, NZ, 2, BLK)
        ids = lax.dynamic_index_in_dim(ids, x, 1, keepdims=False).transpose(0, 2, 1, 3).reshape(NY, 64)
        ids = turned(ids, y)
        start = jnp.sum((response_doc[None, :] < doc[:, None]).astype(jnp.int32), axis=1)
        far = jnp.int32(1 << 20)
        first = jnp.where(y == NY - 1, start, -far)[:, None]
        last = jnp.where(y == NY - 1, ids, far)[:, None]
        at = [x * 512]
        for core in (k, 1 - k):
            at += [((x - d) % NX) * 512 + core * HALF for d in range(1, NX)]
        place_of = jnp.stack(at + [y]).astype(jnp.int32)

        ahead = after(gu[1:], q)
        gu = gu[:1] + [shift(w, "z", NZ, d + 1) for d, w in enumerate(ahead)]
        outs = attention(place_of, q.reshape(NY, 64, QCOLS), first, last, [latent_cache] + mine + other, absorb_key, absorb_value)

    with jax.named_scope("combine"):
        held = stage(outs[0], out_proj)
        outs = [outs[0]] + [shift(o, "y", NY, d + 1) for d, o in enumerate(outs[1:])]

    with jax.named_scope("routing"):
        pick, blend = routing(((y * 2 + k) * NZ * BLK).reshape(1), after([q], outs[0])[0])

    with jax.named_scope("out_projection"):
        own = jnp.stack([k, z])
        head_out = merge(outs)
        keep1, send1, keep2, send2 = project((1, 2), own, head_out, held, residual)
        swap1 = [shift(a, "core", 2, 1) for a in (send1, send2)]
        (head_out,) = after([head_out], send1)
        keep3, send3, keep, send = project((3, 0), own, head_out, held, residual)
        swap2 = [shift(a, "core", 2, 1) for a in (send3, send)]
        keep, *moved = lax.optimization_barrier((keep, *gu[1:]))
        gu = gu[:1] + list(moved)
        part1, part2 = fold([keep1, keep2], swap1)
        (part3,) = fold([keep3], swap2[:1])
        parts = [shift(p, "z", NZ, d + 1) for d, p in enumerate((part1, part2, part3))]
        parts = [keep, swap2[1]] + parts

    with jax.named_scope("dispatch"):
        gain = lax.dynamic_slice_in_dim(norm_gain, z * CHUNK, CHUNK)[None]
        gu_other = [shift(w, "core", 2, 1) for w in after(gu, keep)]
        hidden, rows = spread(parts, gain, pick)
        ahead = after(dn[1:], hidden)
        dn = dn[:1] + [shift(w, "z", NZ, d + 1) for d, w in enumerate(ahead)]
        rows = rows.reshape(EXPERTS, SLOTS, CHUNK)
        rows = lax.all_to_all(rows, ("y", "x"), split_axis=0, concat_axis=0, tiled=True)
        rows = rows.reshape(EROWS, CHUNK)

    with jax.named_scope("experts"):
        rows, *gu_other = lax.optimization_barrier((rows, *gu_other))
        part = gate_up(z.reshape(1), rows, 1.0 / gain, [w for pair in zip(gu, gu_other) for w in pair])
        part, *moved = lax.optimization_barrier((part, *dn[1:]))
        dn = dn[:1] + list(moved)
        dn_other = [shift(w, "core", 2, 1) for w in after(dn, part)]
        part = lax.all_to_all(part, "z", split_axis=0, concat_axis=0, tiled=True)
        inner = inner_act(part)
        inners = [inner] + [shift(inner, "z", NZ, d) for d in range(1, NZ)]
        result = down(inners, [w for pair in zip(dn, dn_other) for w in pair])

    with jax.named_scope("return"):
        back = lax.all_to_all(
            result.reshape(EXPERTS, SLOTS, CHUNK), ("y", "x"), split_axis=0, concat_axis=0, tiled=True
        ).reshape(EROWS, CHUNK)
        mixed = jnp.dot(blend, back.astype(F32), precision=lax.Precision.HIGHEST, preferred_element_type=F32)
        done = (hidden + mixed).astype(BF).reshape(NZ, BLK, CHUNK)
        done = lax.all_to_all(done, "z", split_axis=0, concat_axis=0, tiled=True)
        return done.transpose(1, 0, 2).reshape(BLK, D)


def solution(mesh):
    fine = Mesh(mesh.devices.reshape(NY, NX, NZ, 2), ("y", "x", "z", "core"))
    ctx, head = ("y", "x"), ("z", "core")
    both = ctx + head
    in_specs = (
        P(both, None, None),
        P(ctx, None),
        P(head, None, None),
        P(head, None, None),
        P(head, None),
        P(both, None),
        P(),
        P(both, None),
        P(both, None),
        P(),
        P(ctx, None, head),
        P(ctx, None, head),
        P(ctx, head, None),
    )
    return jax.shard_map(shards, mesh=fine, in_specs=in_specs, out_specs=P(both, None), check_vma=False)
```

```python
import functools

import jax
import jax.numpy as jnp
from jax import lax
from jax.experimental import pallas as pl
from jax.experimental.pallas import tpu as pltpu
from jax.sharding import Mesh
from jax.sharding import PartitionSpec as P

D = 7168
NOPE = 128
ROPE = 64
LAT = 512
VDIM = 128
EXPERTS = 16
TOP = 8
RESP = 1024
PROMPT = 7168
NX = 4
NY = 4
NZ = 4
GRP = 8
BLK = 8
CAP = 6
QCOLS = GRP * (NOPE + ROPE) + 128
KEYS = 2048
HALF = 256
ROWS = 256
CHUNK = D // NZ
SLOTS = NZ * CAP
EROWS = 16 * SLOTS
LOG2E = 1.4426950408889634
BF = jnp.bfloat16
F32 = jnp.float32
HIDE = -1e30


def shift(a, axis, n, d):
    return lax.ppermute(a, axis, [(i, (i + d) % n) for i in range(n)])


def split3(v):
    hi = v.astype(BF).astype(F32)
    mid = (v - hi).astype(BF).astype(F32)
    low = (v - hi - mid).astype(BF).astype(F32)
    return hi, mid, low


def cost(flops=0, nbytes=1):
    return pl.CostEstimate(flops=flops, bytes_accessed=nbytes, transcendentals=0)


def call(kernel, name, out_shape, in_specs, scratch, mib=32, **more):
    return pl.pallas_call(
        kernel,
        out_shape=out_shape,
        in_specs=in_specs,
        scratch_shapes=scratch,
        compiler_params=pltpu.CompilerParams(vmem_limit_bytes=mib * 2**20),
        cost_estimate=cost(),
        name=name,
        **more,
    )


VM = pl.BlockSpec(memory_space=pltpu.VMEM)
SM = pl.BlockSpec(memory_space=pltpu.SMEM)
AT = pl.BlockSpec(memory_space=pltpu.HBM)
PAIR = 2


def attention_kernel(
    pos_ref, q_ref, first_ref, last_ref, c0, c1, c2, c3, s1, s2, s3, ak_ref, av_ref, o0, o1, o2, o3, kv, rp, st, hide, sem
):
    g = pl.program_id(0)
    outs = (o0, o1, o2, o3)

    def query(at):
        blocks = [lax.rem(pos_ref[7] + d, NY) for d in range(NY)]
        return jnp.concatenate([q_ref[b, :, pl.ds(pl.multiple_of(at, 128), 128)] for b in blocks], axis=0)

    @pl.when(g == 0)
    def _():
        copies = [pltpu.make_async_copy(c0, kv.at[pl.ds(pl.multiple_of(pos_ref[0], HALF), 2 * HALF)], sem.at[0])]
        for i, piece in enumerate((c1, c2, c3, s1, s2, s3)):
            to = kv.at[pl.ds(pl.multiple_of(pos_ref[1 + i], HALF), HALF)]
            copies.append(pltpu.make_async_copy(piece, to, sem.at[1 + i]))
        for c in copies:
            c.start()
        col = lax.broadcasted_iota(jnp.int32, (ROWS, KEYS // 2), 1)
        hide[...] = jnp.where((col >= first_ref[...]) & (col <= last_ref[...]), 0.0, HIDE)
        st[...] = jnp.zeros_like(st)
        for c in copies:
            c.wait()
        r = kv[:, LAT:]
        rp[...] = jnp.concatenate([r, r], axis=1)

    lane = lax.broadcasted_iota(jnp.int32, (ROWS, 128), 1)
    nt = (((1,), (1,)), ((), ()))
    step = 512
    scale = LOG2E * (NOPE + ROPE) ** (-0.5)
    scored = []
    for i in range(PAIR):
        h = g * PAIR + i
        nope = query(h * NOPE)
        q_lat = jnp.dot(nope, ak_ref[i], preferred_element_type=F32).astype(BF)
        pair = query(GRP * NOPE + (h // 2) * 128).astype(F32)
        rope = jnp.where(lane // ROPE == h % 2, pair, 0.0).astype(BF)
        parts = []
        for j in range(0, KEYS, step):
            s = lax.dot_general(q_lat, kv[j : j + step, :LAT], nt, preferred_element_type=F32)
            s = s + lax.dot_general(rope, rp[j : j + step, :], nt, preferred_element_type=F32)
            if j >= KEYS // 2:
                s = s + hide[:, j - KEYS // 2 : j - KEYS // 2 + step]
            parts.append(s)
        scored.append(parts)
    for i, parts in enumerate(scored):
        h = g * PAIR + i
        top = jnp.max(parts[0], axis=1, keepdims=True)
        for s in parts[1:]:
            top = jnp.maximum(top, jnp.max(s, axis=1, keepdims=True))
        total = jnp.zeros((ROWS, 1), F32)
        acc = jnp.zeros((ROWS, LAT), F32)
        for n, s in enumerate(parts):
            p = jnp.exp2((s - top) * scale)
            total = total + jnp.sum(p, axis=1, keepdims=True)
            acc = acc + jnp.dot(p.astype(BF), kv[n * step : (n + 1) * step, :LAT], preferred_element_type=F32)
        lat = (acc / total).astype(BF)
        head = jnp.dot(lat, av_ref[i], preferred_element_type=F32).astype(BF)
        for d, o in enumerate(outs):
            o[:, pl.ds(pl.multiple_of(h * VDIM, VDIM), VDIM)] = head[d * 64 : (d + 1) * 64]
        add = jnp.zeros((ROWS, 128), F32)
        for n, v in enumerate(split3(top) + split3(total)):
            add = add + jnp.where(lane == n * GRP + h, v, 0.0)
        st[...] += add

    @pl.when(g == GRP // PAIR - 1)
    def _():
        for d, o in enumerate(outs):
            o[:, GRP * VDIM :] = st[d * 64 : (d + 1) * 64, :].astype(BF)


def attention(place, q, first, last, pieces, absorb_key, absorb_value):
    whole = lambda a: pl.BlockSpec(a.shape, lambda g: (0,) * a.ndim)
    return call(
        attention_kernel,
        "attention",
        (jax.ShapeDtypeStruct((64, GRP * VDIM + 128), BF),) * NY,
        [SM, whole(q), whole(first), whole(last)]
        + [AT] * 7
        + [
            pl.BlockSpec((PAIR, NOPE, LAT), lambda g: (g, 0, 0)),
            pl.BlockSpec((PAIR, LAT, VDIM), lambda g: (g, 0, 0)),
        ],
        [
            pltpu.VMEM((KEYS, LAT + ROPE), BF),
            pltpu.VMEM((KEYS, 2 * ROPE), BF),
            pltpu.VMEM((ROWS, 128), F32),
            pltpu.VMEM((ROWS, KEYS // 2), F32),
            pltpu.SemaphoreType.DMA((7,)),
        ],
        grid=(GRP // PAIR,),
        out_specs=(pl.BlockSpec((64, GRP * VDIM + 128), lambda g: (0, 0)),) * NY,
    )(place, q, first, last, *pieces, absorb_key, absorb_value)


def routing_kernel(at_ref, col_ref, q_ref, pick_ref, blend_ref, held, sem):
    rows = q_ref.at[pl.ds(pl.multiple_of(at_ref[0], NZ * BLK), NZ * BLK), pl.ds(QCOLS - 128, 128)]
    copy = pltpu.make_async_copy(rows, held, sem)
    copy.start()
    copy.wait()
    info = held[...].astype(F32)
    rows = NZ * BLK
    route = info[:, :TOP]
    score = info[:, TOP : 2 * TOP] + info[:, 2 * TOP : 3 * TOP] + info[:, 3 * TOP : 4 * TOP]
    weight = 2.5 * score / jnp.sum(score, axis=1, keepdims=True)
    expert, block, slot = col_ref[0:1, :], col_ref[1:2, :], col_ref[2:3, :]
    named = jnp.zeros((rows, EROWS), F32)
    mix = jnp.zeros((rows, EROWS), F32)
    for n in range(TOP):
        hit = route[:, n : n + 1] == expert
        named = named + jnp.where(hit, 1.0, 0.0)
        mix = mix + jnp.where(hit, weight[:, n : n + 1], 0.0)
    i = lax.broadcasted_iota(jnp.int32, (rows, rows), 0)
    j = lax.broadcasted_iota(jnp.int32, (rows, rows), 1)
    ahead = jnp.where((j < i) & (j // BLK == i // BLK), 1.0, 0.0).astype(BF)
    rank = jnp.dot(ahead, named.astype(BF), preferred_element_type=F32)
    mine = (lax.broadcasted_iota(jnp.int32, (rows, EROWS), 0) // BLK).astype(F32)
    place = (named > 0.5) & (block == mine) & (slot == rank)
    pick_ref[...] = jnp.where(place, 1.0, 0.0).astype(BF)
    blend_ref[...] = jnp.where(place, mix, 0.0)


def routing(at, q):
    col = jnp.arange(EROWS, dtype=jnp.int32)
    cols = jnp.stack([col // SLOTS, col % SLOTS // CAP, col % CAP] + [col * 0] * 5).astype(F32)
    rows = NZ * BLK
    return call(
        routing_kernel,
        "routing",
        (jax.ShapeDtypeStruct((rows, EROWS), BF), jax.ShapeDtypeStruct((rows, EROWS), F32)),
        [SM, VM, AT],
        [pltpu.VMEM((rows, 128), BF), pltpu.SemaphoreType.DMA],
        out_specs=(VM, VM),
    )(at, cols, q)


def merge_kernel(o0, o1, o2, o3, head_out):
    outs = (o0, o1, o2, o3)
    tops, totals = [], []
    for o in outs:
        st = o[:, GRP * VDIM :].astype(F32)
        part = [st[:, n * GRP : (n + 1) * GRP] for n in range(6)]
        tops.append(part[0] + part[1] + part[2])
        totals.append(part[3] + part[4] + part[5])
    top = jnp.maximum(jnp.maximum(tops[0], tops[1]), jnp.maximum(tops[2], tops[3]))
    scale = LOG2E * (NOPE + ROPE) ** (-0.5)
    share = [t * jnp.exp2((m - top) * scale) for m, t in zip(tops, totals)]
    whole = share[0] + share[1] + share[2] + share[3]
    share = [s / whole for s in share]
    for h in range(GRP):
        at = slice(h * VDIM, (h + 1) * VDIM)
        total = sum(o[:, at].astype(F32) * share[s][:, h : h + 1] for s, o in enumerate(outs))
        head_out[:, at] = total.astype(BF)


def merge(outs):
    return call(
        merge_kernel,
        "merge",
        jax.ShapeDtypeStruct((64, GRP * VDIM), BF),
        [VM] * 4,
        [],
        out_specs=VM,
    )(*outs)


def stage_kernel(token_ref, w_ref, held_ref, sem):
    rows = w_ref.shape[0] // 8
    copies = [
        pltpu.make_async_copy(w_ref.at[pl.ds(i * rows, rows)], held_ref.at[pl.ds(i * rows, rows)], sem.at[i])
        for i in range(8)
    ]
    for c in copies:
        c.start()
    for c in copies:
        c.wait()


def stage(token, w):
    return call(
        stage_kernel,
        "stage",
        pltpu.VMEM(w.shape, w.dtype),
        [AT, AT],
        [pltpu.SemaphoreType.DMA((8,))],
        mib=44,
        out_specs=VM,
    )(token, w)


def project_kernel(ways, own_ref, head_ref, w_ref, res_ref, *outs):
    half = NZ * BLK
    for n, d in enumerate(ways):
        keep_ref, send_ref = outs[2 * n], outs[2 * n + 1]
        at = pl.ds(pl.multiple_of(lax.rem(own_ref[1] + d, NZ) * CHUNK, CHUNK), CHUNK)
        part = jnp.dot(head_ref[...], w_ref[:, at], preferred_element_type=F32)
        row = lax.broadcasted_iota(jnp.int32, part.shape, 0) // BLK
        res = jnp.concatenate([res_ref[:, at].astype(F32)] * 8, axis=0)
        part = part + jnp.where(row == own_ref[0] * NZ + own_ref[1], res, 0.0)
        low = jnp.broadcast_to(own_ref[0], (half, CHUNK)) == 0
        keep_ref[...] = jnp.where(low, part[:half], part[half:])
        send_ref[...] = jnp.where(low, part[half:], part[:half]).astype(BF)


def project(ways, own, head_out, out_proj, residual):
    shape = (NZ * BLK, CHUNK)
    return call(
        functools.partial(project_kernel, ways),
        "project",
        (jax.ShapeDtypeStruct(shape, F32), jax.ShapeDtypeStruct(shape, BF)) * len(ways),
        [SM] + [VM] * 3,
        [],
        out_specs=(VM,) * (2 * len(ways)),
    )(own, head_out, out_proj, residual)


def fold_kernel(n, *refs):
    for keep, got, out in zip(refs[:n], refs[n : 2 * n], refs[2 * n :]):
        out[...] = (keep[...] + got[...].astype(F32)).astype(BF)


def fold(keeps, gots):
    n = len(keeps)
    return call(
        functools.partial(fold_kernel, n),
        "fold",
        (jax.ShapeDtypeStruct((NZ * BLK, CHUNK), BF),) * n,
        [VM] * (2 * n),
        [],
        out_specs=(VM,) * n,
    )(*keeps, *gots)


def spread_kernel(keep_ref, got_ref, p1, p2, p3, gain_ref, pick_ref, hidden_ref, rows_ref):
    hidden = keep_ref[...] + got_ref[...].astype(F32) + p1[...].astype(F32) + p2[...].astype(F32) + p3[...].astype(F32)
    hidden_ref[...] = hidden
    scaled = (hidden * gain_ref[...]).astype(BF)
    tn = (((0,), (0,)), ((), ()))
    rows_ref[...] = lax.dot_general(pick_ref[...], scaled, tn, preferred_element_type=F32).astype(BF)


def spread(parts, gain, pick):
    return call(
        spread_kernel,
        "spread",
        (jax.ShapeDtypeStruct((NZ * BLK, CHUNK), F32), pltpu.VMEM((EROWS, CHUNK), BF)),
        [VM] * 7,
        [],
        out_specs=(VM, VM),
    )(*parts, gain, pick)


def gather_kernel(axis, *refs):
    pieces, (held_ref, sem) = refs[:8], refs[8:]
    n = pieces[0].shape[axis]
    copies = []
    for i, p in enumerate(pieces):
        to = held_ref.at[:, pl.ds(i * n, n)] if axis else held_ref.at[pl.ds(i * n, n)]
        copies.append(pltpu.make_async_copy(p, to, sem.at[i]))
    for c in copies:
        c.start()
    for c in copies:
        c.wait()


def gather(axis, name, pieces):
    shape = list(pieces[0].shape)
    shape[axis] *= 8
    return call(
        functools.partial(gather_kernel, axis),
        name,
        pltpu.VMEM(tuple(shape), BF),
        [AT] * 8,
        [pltpu.SemaphoreType.DMA((8,))],
        mib=16,
        out_specs=VM,
    )(*pieces)


def gate_up_kernel(z_ref, x_ref, gain_ref, w, o_ref):
    x = x_ref[...]
    raw = x.astype(F32) * gain_ref[...]
    ones = jnp.ones((8, CHUNK), BF)
    square = lax.dot_general(
        ones, (raw * raw).astype(BF), (((1,), (1,)), ((), ())), preferred_element_type=F32
    )
    row = lax.broadcasted_iota(jnp.int32, square.shape, 0)
    hi, mid, low = split3(square)
    coded = jnp.where(row == 0, hi, jnp.where(row == 1, mid, jnp.where(row == 2, low, 0.0)))
    coded = jnp.concatenate([coded, jnp.zeros_like(coded)], axis=0).astype(BF)
    coded = jnp.concatenate([coded, jnp.zeros((16, 512 - EROWS), BF)], axis=1)
    for d in range(NZ):
        part = jnp.dot(x, w[:, d * 512 : (d + 1) * 512], preferred_element_type=F32).astype(BF)
        to = lax.rem(z_ref[0] + NZ - d, NZ)
        o_ref[to, :EROWS] = part
        o_ref[to, EROWS:] = coded


def gate_up(z, x, gain, held):
    return call(
        gate_up_kernel,
        "gate_up",
        pltpu.VMEM((NZ, EROWS + 16, 512), BF),
        [SM] + [VM] * 3,
        [],
        out_specs=VM,
    )(z, x, gain, held)


def inner_kernel(part_ref, out_ref):
    total = part_ref[0].astype(F32)
    for s in range(1, NZ):
        total = total + part_ref[s].astype(F32)
    square = jnp.sum(total[EROWS : EROWS + 8], axis=0, keepdims=True)
    scale = lax.rsqrt(jnp.broadcast_to(square[:, :EROWS], (8, EROWS)) / D + 1e-6).T[:, :1]
    total = total[:EROWS] * scale
    for k in range(2):
        gate, up = total[:, k * 256 : k * 256 + 128], total[:, k * 256 + 128 : k * 256 + 256]
        out_ref[:, k * 128 : (k + 1) * 128] = (gate / (1.0 + jnp.exp(-gate)) * up).astype(BF)


def inner_act(part):
    return call(inner_kernel, "inner_act", jax.ShapeDtypeStruct((EROWS, 256), BF), [VM], [], out_specs=VM)(part)


def down_kernel(i0, i1, i2, i3, w, o_ref):
    inner = jnp.concatenate([i0[...], i1[...], i2[...], i3[...]], axis=1)
    o_ref[...] = jnp.dot(inner, w[...], preferred_element_type=F32).astype(BF)


def down(inners, held):
    return call(
        down_kernel,
        "down",
        pltpu.VMEM((EROWS, CHUNK), BF),
        [VM] * 5,
        [],
        out_specs=VM,
    )(*inners, held)


def after(arrays, token):
    out = lax.optimization_barrier(tuple(arrays) + (token,))
    return out[:-1]


def turned(a, by):
    return lax.dynamic_slice_in_dim(jnp.concatenate([a, a]), by, a.shape[0], axis=0).reshape(-1)


def shards(
    queries,
    latent_cache,
    absorb_key,
    absorb_value,
    out_proj,
    residual,
    norm_gain,
    routes,
    route_score,
    response_doc,
    expert_gate,
    expert_up,
    expert_down,
):
    x, y, z, k = (lax.axis_index(a) for a in ("x", "y", "z", "core"))

    with jax.named_scope("cache_gather"):
        half = lax.dynamic_slice_in_dim(latent_cache, k * HALF, HALF, axis=0)
        mine = [shift(half, "x", NX, d) for d in range(1, NX)]

    with jax.named_scope("query_exchange"):
        score_hi = lax.reduce_precision(route_score, 8, 7)
        score_mid = lax.reduce_precision(route_score - score_hi, 8, 7)
        score_low = route_score - score_hi - score_mid
        info = jnp.concatenate(
            [routes.astype(BF)]
            + [s.astype(BF) for s in (score_hi, score_mid, score_low)]
            + [jnp.zeros((BLK, 128 - 4 * TOP), BF)],
            axis=1,
        )
        info = jnp.broadcast_to(info[:, None, None], (BLK, NZ, 2, 128))
        nope = queries[:, :, :NOPE].reshape(BLK, NZ, 2, GRP * NOPE)
        rope = queries[:, :, NOPE:].reshape(BLK, NZ, 2, GRP * ROPE)
        q = jnp.concatenate([nope, rope, info], axis=3).transpose(2, 1, 0, 3)
        q = jnp.broadcast_to(q[None], (NY, 2, NZ, BLK, QCOLS))
        q = q.reshape(NY * 2 * NZ, BLK, QCOLS)
        (q,) = after([q], mine[0])
        q = lax.all_to_all(q, ("y", "core", "z"), split_axis=0, concat_axis=0, tiled=True)
        q = q.reshape(ROWS, QCOLS)

    with jax.named_scope("weights"):
        gates = expert_gate[0].reshape(NZ, CHUNK, 128)
        ups = expert_up[0].reshape(NZ, CHUNK, 128)
        downs = expert_down[0]
        gu, dn = [], []
        for d in range(NZ):
            to = (z + d) % NZ
            g = lax.dynamic_index_in_dim(gates, to, 0, keepdims=False)
            u = lax.dynamic_index_in_dim(ups, to, 0, keepdims=False)
            gu.append(jnp.concatenate([g, u], axis=1))
            dn.append(lax.dynamic_slice_in_dim(downs, to * CHUNK, CHUNK, axis=1))
    with jax.named_scope("cache_share"):
        other = [shift(m, "core", 2, 1) for m in mine]

    with jax.named_scope("attention"):
        doc = lax.dynamic_index_in_dim(response_doc.reshape(NY, NX, NZ, 2, BLK), x, 1, keepdims=False)
        doc = turned(doc.transpose(0, 2, 1, 3).reshape(NY, 64), y)
        ids = jnp.arange(RESP, dtype=jnp.int32).reshape(NY, NX, NZ, 2, BLK)
        ids = lax.dynamic_index_in_dim(ids, x, 1, keepdims=False).transpose(0, 2, 1, 3).reshape(NY, 64)
        ids = turned(ids, y)
        start = jnp.sum((response_doc[None, :] < doc[:, None]).astype(jnp.int32), axis=1)
        far = jnp.int32(1 << 20)
        first = jnp.where(y == NY - 1, start, -far)[:, None]
        last = jnp.where(y == NY - 1, ids, far)[:, None]
        at = [x * 512]
        for core in (k, 1 - k):
            at += [((x - d) % NX) * 512 + core * HALF for d in range(1, NX)]
        place_of = jnp.stack(at + [y]).astype(jnp.int32)

        ahead = after(gu[1:], q)
        gu = gu[:1] + [shift(w, "z", NZ, d + 1) for d, w in enumerate(ahead)]
        outs = attention(place_of, q.reshape(NY, 64, QCOLS), first, last, [latent_cache] + mine + other, absorb_key, absorb_value)

    with jax.named_scope("combine"):
        held = stage(outs[0], out_proj)
        outs = [outs[0]] + [shift(o, "y", NY, d + 1) for d, o in enumerate(outs[1:])]

    with jax.named_scope("routing"):
        pick, blend = routing(((y * 2 + k) * NZ * BLK).reshape(1), after([q], outs[0])[0])

    with jax.named_scope("out_projection"):
        own = jnp.stack([k, z])
        head_out = merge(outs)
        keep1, send1, keep2, send2 = project((1, 2), own, head_out, held, residual)
        swap1 = [shift(a, "core", 2, 1) for a in (send1, send2)]
        (head_out,) = after([head_out], send1)
        keep3, send3, keep, send = project((3, 0), own, head_out, held, residual)
        swap2 = [shift(a, "core", 2, 1) for a in (send3, send)]
        keep, *moved = lax.optimization_barrier((keep, *gu[1:]))
        gu = gu[:1] + list(moved)
        part1, part2 = fold([keep1, keep2], swap1)
        (part3,) = fold([keep3], swap2[:1])
        parts = [shift(p, "z", NZ, d + 1) for d, p in enumerate((part1, part2, part3))]
        parts = [keep, swap2[1]] + parts

    with jax.named_scope("dispatch"):
        gain = lax.dynamic_slice_in_dim(norm_gain, z * CHUNK, CHUNK)[None]
        gu_other = [shift(w, "core", 2, 1) for w in after(gu, keep)]
        hidden, rows = spread(parts, gain, pick)
        ahead = after(dn[1:], hidden)
        dn = dn[:1] + [shift(w, "z", NZ, d + 1) for d, w in enumerate(ahead)]
        rows = rows.reshape(EXPERTS, SLOTS, CHUNK)
        rows = lax.all_to_all(rows, ("y", "x"), split_axis=0, concat_axis=0, tiled=True)
        rows = rows.reshape(EROWS, CHUNK)

    with jax.named_scope("experts"):
        held = gather(1, "gate_up_weights", [w for pair in zip(gu, gu_other) for w in pair])
        part = gate_up(z.reshape(1), rows, 1.0 / gain, held)
        part, *moved = lax.optimization_barrier((part, *dn[1:]))
        dn = dn[:1] + list(moved)
        dn_other = [shift(w, "core", 2, 1) for w in after(dn, part)]
        part = lax.all_to_all(part, "z", split_axis=0, concat_axis=0, tiled=True)
        inner = inner_act(part)
        inners = [inner] + [shift(inner, "z", NZ, d) for d in range(1, NZ)]
        held = gather(0, "down_weights", [w for pair in zip(dn, dn_other) for w in pair])
        result = down(inners, held)

    with jax.named_scope("return"):
        back = lax.all_to_all(
            result.reshape(EXPERTS, SLOTS, CHUNK), ("y", "x"), split_axis=0, concat_axis=0, tiled=True
        ).reshape(EROWS, CHUNK)
        mixed = jnp.dot(blend, back.astype(F32), precision=lax.Precision.HIGHEST, preferred_element_type=F32)
        done = (hidden + mixed).astype(BF).reshape(NZ, BLK, CHUNK)
        done = lax.all_to_all(done, "z", split_axis=0, concat_axis=0, tiled=True)
        return done.transpose(1, 0, 2).reshape(BLK, D)


def solution(mesh):
    fine = Mesh(mesh.devices.reshape(NY, NX, NZ, 2), ("y", "x", "z", "core"))
    ctx, head = ("y", "x"), ("z", "core")
    both = ctx + head
    in_specs = (
        P(both, None, None),
        P(ctx, None),
        P(head, None, None),
        P(head, None, None),
        P(head, None),
        P(both, None),
        P(),
        P(both, None),
        P(both, None),
        P(),
        P(ctx, None, head),
        P(ctx, None, head),
        P(ctx, head, None),
    )
    return jax.shard_map(shards, mesh=fine, in_specs=in_specs, out_specs=P(both, None), check_vma=False)
```

```python
import functools

import jax
import jax.numpy as jnp
from jax import lax
from jax.experimental import pallas as pl
from jax.experimental.pallas import tpu as pltpu
from jax.sharding import Mesh
from jax.sharding import PartitionSpec as P

D = 7168
NOPE = 128
ROPE = 64
LAT = 512
VDIM = 128
EXPERTS = 16
TOP = 8
RESP = 1024
PROMPT = 7168
NX = 4
NY = 4
NZ = 4
GRP = 8
BLK = 8
CAP = 6
QCOLS = GRP * (NOPE + ROPE) + 128
KEYS = 2048
HALF = 256
ROWS = 256
CHUNK = D // NZ
SLOTS = NZ * CAP
EROWS = 16 * SLOTS
LOG2E = 1.4426950408889634
BF = jnp.bfloat16
F32 = jnp.float32
HIDE = -1e30


def shift(a, axis, n, d):
    return lax.ppermute(a, axis, [(i, (i + d) % n) for i in range(n)])


def split3(v):
    hi = v.astype(BF).astype(F32)
    mid = (v - hi).astype(BF).astype(F32)
    low = (v - hi - mid).astype(BF).astype(F32)
    return hi, mid, low


def cost(flops=0, nbytes=1):
    return pl.CostEstimate(flops=flops, bytes_accessed=nbytes, transcendentals=0)


def call(kernel, name, out_shape, in_specs, scratch, mib=32, **more):
    return pl.pallas_call(
        kernel,
        out_shape=out_shape,
        in_specs=in_specs,
        scratch_shapes=scratch,
        compiler_params=pltpu.CompilerParams(vmem_limit_bytes=mib * 2**20),
        cost_estimate=cost(),
        name=name,
        **more,
    )


VM = pl.BlockSpec(memory_space=pltpu.VMEM)
SM = pl.BlockSpec(memory_space=pltpu.SMEM)
AT = pl.BlockSpec(memory_space=pltpu.HBM)
PAIR = 2


def attention_kernel(
    pos_ref, q_ref, first_ref, last_ref, c0, c1, c2, c3, s1, s2, s3, ak_ref, av_ref, o0, o1, o2, o3, kv, rp, st, hide, sem
):
    g = pl.program_id(0)
    outs = (o0, o1, o2, o3)

    def query(at):
        blocks = [lax.rem(pos_ref[7] + d, NY) for d in range(NY)]
        return jnp.concatenate([q_ref[b, :, pl.ds(pl.multiple_of(at, 128), 128)] for b in blocks], axis=0)

    @pl.when(g == 0)
    def _():
        copies = [pltpu.make_async_copy(c0, kv.at[pl.ds(pl.multiple_of(pos_ref[0], HALF), 2 * HALF)], sem.at[0])]
        for i, piece in enumerate((c1, c2, c3, s1, s2, s3)):
            to = kv.at[pl.ds(pl.multiple_of(pos_ref[1 + i], HALF), HALF)]
            copies.append(pltpu.make_async_copy(piece, to, sem.at[1 + i]))
        for c in copies:
            c.start()
        col = lax.broadcasted_iota(jnp.int32, (ROWS, KEYS // 2), 1)
        hide[...] = jnp.where((col >= first_ref[...]) & (col <= last_ref[...]), 0.0, HIDE)
        st[...] = jnp.zeros_like(st)
        for c in copies:
            c.wait()
        r = kv[:, LAT:]
        rp[...] = jnp.concatenate([r, r], axis=1)

    lane = lax.broadcasted_iota(jnp.int32, (ROWS, 128), 1)
    nt = (((1,), (1,)), ((), ()))
    step = 512
    scale = LOG2E * (NOPE + ROPE) ** (-0.5)
    scored = []
    for i in range(PAIR):
        h = g * PAIR + i
        nope = query(h * NOPE)
        q_lat = jnp.dot(nope, ak_ref[i], preferred_element_type=F32).astype(BF)
        pair = query(GRP * NOPE + (h // 2) * 128).astype(F32)
        rope = jnp.where(lane // ROPE == h % 2, pair, 0.0).astype(BF)
        parts = []
        for j in range(0, KEYS, step):
            s = lax.dot_general(q_lat, kv[j : j + step, :LAT], nt, preferred_element_type=F32)
            s = s + lax.dot_general(rope, rp[j : j + step, :], nt, preferred_element_type=F32)
            if j >= KEYS // 2:
                s = s + hide[:, j - KEYS // 2 : j - KEYS // 2 + step]
            parts.append(s)
        scored.append(parts)
    for i, parts in enumerate(scored):
        h = g * PAIR + i
        top = jnp.max(parts[0], axis=1, keepdims=True)
        for s in parts[1:]:
            top = jnp.maximum(top, jnp.max(s, axis=1, keepdims=True))
        total = jnp.zeros((ROWS, 1), F32)
        acc = jnp.zeros((ROWS, LAT), F32)
        for n, s in enumerate(parts):
            p = jnp.exp2((s - top) * scale)
            total = total + jnp.sum(p, axis=1, keepdims=True)
            acc = acc + jnp.dot(p.astype(BF), kv[n * step : (n + 1) * step, :LAT], preferred_element_type=F32)
        lat = (acc / total).astype(BF)
        head = jnp.dot(lat, av_ref[i], preferred_element_type=F32).astype(BF)
        for d, o in enumerate(outs):
            o[:, pl.ds(pl.multiple_of(h * VDIM, VDIM), VDIM)] = head[d * 64 : (d + 1) * 64]
        add = jnp.zeros((ROWS, 128), F32)
        for n, v in enumerate(split3(top) + split3(total)):
            add = add + jnp.where(lane == n * GRP + h, v, 0.0)
        st[...] += add

    @pl.when(g == GRP // PAIR - 1)
    def _():
        for d, o in enumerate(outs):
            o[:, GRP * VDIM :] = st[d * 64 : (d + 1) * 64, :].astype(BF)


def attention(place, q, first, last, pieces, absorb_key, absorb_value):
    whole = lambda a: pl.BlockSpec(a.shape, lambda g: (0,) * a.ndim)
    return call(
        attention_kernel,
        "attention",
        (jax.ShapeDtypeStruct((64, GRP * VDIM + 128), BF),) * NY,
        [SM, whole(q), whole(first), whole(last)]
        + [AT] * 7
        + [
            pl.BlockSpec((PAIR, NOPE, LAT), lambda g: (g, 0, 0)),
            pl.BlockSpec((PAIR, LAT, VDIM), lambda g: (g, 0, 0)),
        ],
        [
            pltpu.VMEM((KEYS, LAT + ROPE), BF),
            pltpu.VMEM((KEYS, 2 * ROPE), BF),
            pltpu.VMEM((ROWS, 128), F32),
            pltpu.VMEM((ROWS, KEYS // 2), F32),
            pltpu.SemaphoreType.DMA((7,)),
        ],
        grid=(GRP // PAIR,),
        out_specs=(pl.BlockSpec((64, GRP * VDIM + 128), lambda g: (0, 0)),) * NY,
    )(place, q, first, last, *pieces, absorb_key, absorb_value)


def routing_kernel(at_ref, col_ref, q_ref, pick_ref, blend_ref, held, sem):
    rows = q_ref.at[pl.ds(pl.multiple_of(at_ref[0], NZ * BLK), NZ * BLK), pl.ds(QCOLS - 128, 128)]
    copy = pltpu.make_async_copy(rows, held, sem)
    copy.start()
    copy.wait()
    info = held[...].astype(F32)
    rows = NZ * BLK
    route = info[:, :TOP]
    score = info[:, TOP : 2 * TOP] + info[:, 2 * TOP : 3 * TOP] + info[:, 3 * TOP : 4 * TOP]
    weight = 2.5 * score / jnp.sum(score, axis=1, keepdims=True)
    expert, block, slot = col_ref[0:1, :], col_ref[1:2, :], col_ref[2:3, :]
    named = jnp.zeros((rows, EROWS), F32)
    mix = jnp.zeros((rows, EROWS), F32)
    for n in range(TOP):
        hit = route[:, n : n + 1] == expert
        named = named + jnp.where(hit, 1.0, 0.0)
        mix = mix + jnp.where(hit, weight[:, n : n + 1], 0.0)
    i = lax.broadcasted_iota(jnp.int32, (rows, rows), 0)
    j = lax.broadcasted_iota(jnp.int32, (rows, rows), 1)
    ahead = jnp.where((j < i) & (j // BLK == i // BLK), 1.0, 0.0).astype(BF)
    rank = jnp.dot(ahead, named.astype(BF), preferred_element_type=F32)
    mine = (lax.broadcasted_iota(jnp.int32, (rows, EROWS), 0) // BLK).astype(F32)
    place = (named > 0.5) & (block == mine) & (slot == rank)
    pick_ref[...] = jnp.where(place, 1.0, 0.0).astype(BF)
    blend_ref[...] = jnp.where(place, mix, 0.0)


def routing(at, q):
    col = jnp.arange(EROWS, dtype=jnp.int32)
    cols = jnp.stack([col // SLOTS, col % SLOTS // CAP, col % CAP] + [col * 0] * 5).astype(F32)
    rows = NZ * BLK
    return call(
        routing_kernel,
        "routing",
        (jax.ShapeDtypeStruct((rows, EROWS), BF), jax.ShapeDtypeStruct((rows, EROWS), F32)),
        [SM, VM, AT],
        [pltpu.VMEM((rows, 128), BF), pltpu.SemaphoreType.DMA],
        out_specs=(VM, VM),
    )(at, cols, q)


def merge_kernel(o0, o1, o2, o3, head_out):
    outs = (o0, o1, o2, o3)
    tops, totals = [], []
    for o in outs:
        st = o[:, GRP * VDIM :].astype(F32)
        part = [st[:, n * GRP : (n + 1) * GRP] for n in range(6)]
        tops.append(part[0] + part[1] + part[2])
        totals.append(part[3] + part[4] + part[5])
    top = jnp.maximum(jnp.maximum(tops[0], tops[1]), jnp.maximum(tops[2], tops[3]))
    scale = LOG2E * (NOPE + ROPE) ** (-0.5)
    share = [t * jnp.exp2((m - top) * scale) for m, t in zip(tops, totals)]
    whole = share[0] + share[1] + share[2] + share[3]
    share = [s / whole for s in share]
    for h in range(GRP):
        at = slice(h * VDIM, (h + 1) * VDIM)
        total = sum(o[:, at].astype(F32) * share[s][:, h : h + 1] for s, o in enumerate(outs))
        head_out[:, at] = total.astype(BF)


def merge(outs):
    return call(
        merge_kernel,
        "merge",
        jax.ShapeDtypeStruct((64, GRP * VDIM), BF),
        [VM] * 4,
        [],
        out_specs=VM,
    )(*outs)


def stage_kernel(token_ref, w_ref, held_ref, sem):
    rows = w_ref.shape[0] // 8
    copies = [
        pltpu.make_async_copy(w_ref.at[pl.ds(i * rows, rows)], held_ref.at[pl.ds(i * rows, rows)], sem.at[i])
        for i in range(8)
    ]
    for c in copies:
        c.start()
    for c in copies:
        c.wait()


def stage(token, w):
    return call(
        stage_kernel,
        "stage",
        pltpu.VMEM(w.shape, w.dtype),
        [AT, AT],
        [pltpu.SemaphoreType.DMA((8,))],
        mib=44,
        out_specs=VM,
    )(token, w)


def project_kernel(ways, own_ref, head_ref, w_ref, res_ref, *outs):
    half = NZ * BLK
    for n, d in enumerate(ways):
        keep_ref, send_ref = outs[2 * n], outs[2 * n + 1]
        at = pl.ds(pl.multiple_of(lax.rem(own_ref[1] + d, NZ) * CHUNK, CHUNK), CHUNK)
        part = jnp.dot(head_ref[...], w_ref[:, at], preferred_element_type=F32)
        row = lax.broadcasted_iota(jnp.int32, part.shape, 0) // BLK
        res = jnp.concatenate([res_ref[:, at].astype(F32)] * 8, axis=0)
        part = part + jnp.where(row == own_ref[0] * NZ + own_ref[1], res, 0.0)
        low = jnp.broadcast_to(own_ref[0], (half, CHUNK)) == 0
        keep_ref[...] = jnp.where(low, part[:half], part[half:])
        send_ref[...] = jnp.where(low, part[half:], part[:half]).astype(BF)


def project(ways, own, head_out, out_proj, residual):
    shape = (NZ * BLK, CHUNK)
    return call(
        functools.partial(project_kernel, ways),
        "project",
        (jax.ShapeDtypeStruct(shape, F32), jax.ShapeDtypeStruct(shape, BF)) * len(ways),
        [SM] + [VM] * 3,
        [],
        out_specs=(VM,) * (2 * len(ways)),
    )(own, head_out, out_proj, residual)


def fold_kernel(n, *refs):
    for keep, got, out in zip(refs[:n], refs[n : 2 * n], refs[2 * n :]):
        out[...] = (keep[...] + got[...].astype(F32)).astype(BF)


def fold(keeps, gots):
    n = len(keeps)
    return call(
        functools.partial(fold_kernel, n),
        "fold",
        (jax.ShapeDtypeStruct((NZ * BLK, CHUNK), BF),) * n,
        [VM] * (2 * n),
        [],
        out_specs=(VM,) * n,
    )(*keeps, *gots)


def spread_kernel(keep_ref, got_ref, p1, p2, p3, gain_ref, pick_ref, hidden_ref, rows_ref):
    hidden = keep_ref[...] + got_ref[...].astype(F32) + p1[...].astype(F32) + p2[...].astype(F32) + p3[...].astype(F32)
    hidden_ref[...] = hidden
    scaled = (hidden * gain_ref[...]).astype(BF)
    tn = (((0,), (0,)), ((), ()))
    rows_ref[...] = lax.dot_general(pick_ref[...], scaled, tn, preferred_element_type=F32).astype(BF)


def spread(parts, gain, pick):
    return call(
        spread_kernel,
        "spread",
        (jax.ShapeDtypeStruct((NZ * BLK, CHUNK), F32), pltpu.VMEM((EROWS, CHUNK), BF)),
        [VM] * 7,
        [],
        out_specs=(VM, VM),
    )(*parts, gain, pick)


def gather_kernel(*refs):
    pieces, (held_ref, sem) = refs[:8], refs[8:]
    n = pieces[0].shape[0]
    copies = [pltpu.make_async_copy(p, held_ref.at[pl.ds(i * n, n)], sem.at[i]) for i, p in enumerate(pieces)]
    for c in copies:
        c.start()
    for c in copies:
        c.wait()


def gather(pieces):
    return call(
        gather_kernel,
        "down_weights",
        pltpu.VMEM((1024, CHUNK), BF),
        [AT] * 8,
        [pltpu.SemaphoreType.DMA((8,))],
        mib=16,
        out_specs=VM,
    )(*pieces)


def gate_up_kernel(z_ref, x_ref, gain_ref, *refs):
    pieces, (o_ref, w, sem) = refs[:8], refs[8:]
    copies = [
        pltpu.make_async_copy(p, w.at[:, pl.ds(i * 256, 256)], sem.at[i]) for i, p in enumerate(pieces)
    ]
    for c in copies:
        c.start()
    x = x_ref[...]
    raw = x.astype(F32) * gain_ref[...]
    ones = jnp.ones((8, CHUNK), BF)
    square = lax.dot_general(
        ones, (raw * raw).astype(BF), (((1,), (1,)), ((), ())), preferred_element_type=F32
    )
    row = lax.broadcasted_iota(jnp.int32, square.shape, 0)
    hi, mid, low = split3(square)
    coded = jnp.where(row == 0, hi, jnp.where(row == 1, mid, jnp.where(row == 2, low, 0.0)))
    coded = jnp.concatenate([coded, jnp.zeros_like(coded)], axis=0).astype(BF)
    coded = jnp.concatenate([coded, jnp.zeros((16, 512 - EROWS), BF)], axis=1)
    for d in range(NZ):
        copies[2 * d].wait()
        copies[2 * d + 1].wait()
        part = jnp.dot(x, w[:, d * 512 : (d + 1) * 512], preferred_element_type=F32).astype(BF)
        to = lax.rem(z_ref[0] + NZ - d, NZ)
        o_ref[to, :EROWS] = part
        o_ref[to, EROWS:] = coded


def gate_up(z, x, gain, pieces):
    return call(
        gate_up_kernel,
        "gate_up",
        pltpu.VMEM((NZ, EROWS + 16, 512), BF),
        [SM, VM, VM] + [AT] * 8,
        [pltpu.VMEM((CHUNK, 2048), BF), pltpu.SemaphoreType.DMA((8,))],
        out_specs=VM,
    )(z, x, gain, *pieces)


def inner_kernel(part_ref, out_ref):
    total = part_ref[0].astype(F32)
    for s in range(1, NZ):
        total = total + part_ref[s].astype(F32)
    square = jnp.sum(total[EROWS : EROWS + 8], axis=0, keepdims=True)
    scale = lax.rsqrt(jnp.broadcast_to(square[:, :EROWS], (8, EROWS)) / D + 1e-6).T[:, :1]
    total = total[:EROWS] * scale
    for k in range(2):
        gate, up = total[:, k * 256 : k * 256 + 128], total[:, k * 256 + 128 : k * 256 + 256]
        out_ref[:, k * 128 : (k + 1) * 128] = (gate / (1.0 + jnp.exp(-gate)) * up).astype(BF)


def inner_act(part):
    return call(inner_kernel, "inner_act", jax.ShapeDtypeStruct((EROWS, 256), BF), [VM], [], out_specs=VM)(part)


def down_kernel(i0, i1, i2, i3, w, o_ref):
    inner = jnp.concatenate([i0[...], i1[...], i2[...], i3[...]], axis=1)
    o_ref[...] = jnp.dot(inner, w[...], preferred_element_type=F32).astype(BF)


def down(inners, held):
    return call(
        down_kernel,
        "down",
        pltpu.VMEM((EROWS, CHUNK), BF),
        [VM] * 5,
        [],
        out_specs=VM,
    )(*inners, held)


def after(arrays, token):
    out = lax.optimization_barrier(tuple(arrays) + (token,))
    return out[:-1]


def turned(a, by):
    return lax.dynamic_slice_in_dim(jnp.concatenate([a, a]), by, a.shape[0], axis=0).reshape(-1)


def shards(
    queries,
    latent_cache,
    absorb_key,
    absorb_value,
    out_proj,
    residual,
    norm_gain,
    routes,
    route_score,
    response_doc,
    expert_gate,
    expert_up,
    expert_down,
):
    x, y, z, k = (lax.axis_index(a) for a in ("x", "y", "z", "core"))

    with jax.named_scope("cache_gather"):
        half = lax.dynamic_slice_in_dim(latent_cache, k * HALF, HALF, axis=0)
        mine = [shift(half, "x", NX, d) for d in range(1, NX)]

    with jax.named_scope("query_exchange"):
        score_hi = lax.reduce_precision(route_score, 8, 7)
        score_mid = lax.reduce_precision(route_score - score_hi, 8, 7)
        score_low = route_score - score_hi - score_mid
        info = jnp.concatenate(
            [routes.astype(BF)]
            + [s.astype(BF) for s in (score_hi, score_mid, score_low)]
            + [jnp.zeros((BLK, 128 - 4 * TOP), BF)],
            axis=1,
        )
        info = jnp.broadcast_to(info[:, None, None], (BLK, NZ, 2, 128))
        nope = queries[:, :, :NOPE].reshape(BLK, NZ, 2, GRP * NOPE)
        rope = queries[:, :, NOPE:].reshape(BLK, NZ, 2, GRP * ROPE)
        q = jnp.concatenate([nope, rope, info], axis=3).transpose(2, 1, 0, 3)
        q = jnp.broadcast_to(q[None], (NY, 2, NZ, BLK, QCOLS))
        q = q.reshape(NY * 2 * NZ, BLK, QCOLS)
        (q,) = after([q], mine[0])
        q = lax.all_to_all(q, ("y", "core", "z"), split_axis=0, concat_axis=0, tiled=True)
        q = q.reshape(ROWS, QCOLS)

    with jax.named_scope("weights"):
        gates = expert_gate[0].reshape(NZ, CHUNK, 128)
        ups = expert_up[0].reshape(NZ, CHUNK, 128)
        downs = expert_down[0]
        gu, dn = [], []
        for d in range(NZ):
            to = (z + d) % NZ
            g = lax.dynamic_index_in_dim(gates, to, 0, keepdims=False)
            u = lax.dynamic_index_in_dim(ups, to, 0, keepdims=False)
            gu.append(jnp.concatenate([g, u], axis=1))
            dn.append(lax.dynamic_slice_in_dim(downs, to * CHUNK, CHUNK, axis=1))
    with jax.named_scope("cache_share"):
        other = [shift(m, "core", 2, 1) for m in mine]

    with jax.named_scope("attention"):
        doc = lax.dynamic_index_in_dim(response_doc.reshape(NY, NX, NZ, 2, BLK), x, 1, keepdims=False)
        doc = turned(doc.transpose(0, 2, 1, 3).reshape(NY, 64), y)
        ids = jnp.arange(RESP, dtype=jnp.int32).reshape(NY, NX, NZ, 2, BLK)
        ids = lax.dynamic_index_in_dim(ids, x, 1, keepdims=False).transpose(0, 2, 1, 3).reshape(NY, 64)
        ids = turned(ids, y)
        start = jnp.sum((response_doc[None, :] < doc[:, None]).astype(jnp.int32), axis=1)
        far = jnp.int32(1 << 20)
        first = jnp.where(y == NY - 1, start, -far)[:, None]
        last = jnp.where(y == NY - 1, ids, far)[:, None]
        at = [x * 512]
        for core in (k, 1 - k):
            at += [((x - d) % NX) * 512 + core * HALF for d in range(1, NX)]
        place_of = jnp.stack(at + [y]).astype(jnp.int32)

        ahead = after(gu[1:], q)
        gu = gu[:1] + [shift(w, "z", NZ, d + 1) for d, w in enumerate(ahead)]
        outs = attention(place_of, q.reshape(NY, 64, QCOLS), first, last, [latent_cache] + mine + other, absorb_key, absorb_value)

    with jax.named_scope("combine"):
        held = stage(outs[0], out_proj)
        outs = [outs[0]] + [shift(o, "y", NY, d + 1) for d, o in enumerate(outs[1:])]

    with jax.named_scope("routing"):
        pick, blend = routing(((y * 2 + k) * NZ * BLK).reshape(1), after([q], outs[0])[0])

    with jax.named_scope("out_projection"):
        own = jnp.stack([k, z])
        head_out = merge(outs)
        keep1, send1, keep2, send2 = project((1, 2), own, head_out, held, residual)
        swap1 = [shift(a, "core", 2, 1) for a in (send1, send2)]
        (head_out,) = after([head_out], send1)
        keep3, send3, keep, send = project((3, 0), own, head_out, held, residual)
        swap2 = [shift(a, "core", 2, 1) for a in (send3, send)]
        keep, *moved = lax.optimization_barrier((keep, *gu[1:]))
        gu = gu[:1] + list(moved)
        part1, part2 = fold([keep1, keep2], swap1)
        (part3,) = fold([keep3], swap2[:1])
        parts = [shift(p, "z", NZ, d + 1) for d, p in enumerate((part1, part2, part3))]
        parts = [keep, swap2[1]] + parts

    with jax.named_scope("dispatch"):
        gain = lax.dynamic_slice_in_dim(norm_gain, z * CHUNK, CHUNK)[None]
        gu_other = [shift(w, "core", 2, 1) for w in after(gu, keep)]
        hidden, rows = spread(parts, gain, pick)
        ahead = after(dn[1:], hidden)
        dn = dn[:1] + [shift(w, "z", NZ, d + 1) for d, w in enumerate(ahead)]
        rows = rows.reshape(EXPERTS, SLOTS, CHUNK)
        rows = lax.all_to_all(rows, ("y", "x"), split_axis=0, concat_axis=0, tiled=True)
        rows = rows.reshape(EROWS, CHUNK)

    with jax.named_scope("experts"):
        rows, *gu_other = lax.optimization_barrier((rows, *gu_other))
        part = gate_up(z.reshape(1), rows, 1.0 / gain, [w for pair in zip(gu, gu_other) for w in pair])
        part, *moved = lax.optimization_barrier((part, *dn[1:]))
        dn = dn[:1] + list(moved)
        dn_other = [shift(w, "core", 2, 1) for w in after(dn, part)]
        part = lax.all_to_all(part, "z", split_axis=0, concat_axis=0, tiled=True)
        inner = inner_act(part)
        inners = [inner] + [shift(inner, "z", NZ, d) for d in range(1, NZ)]
        held = gather([w for pair in zip(dn, dn_other) for w in pair])
        result = down(inners, held)

    with jax.named_scope("return"):
        back = lax.all_to_all(
            result.reshape(EXPERTS, SLOTS, CHUNK), ("y", "x"), split_axis=0, concat_axis=0, tiled=True
        ).reshape(EROWS, CHUNK)
        mixed = jnp.dot(blend, back.astype(F32), precision=lax.Precision.HIGHEST, preferred_element_type=F32)
        done = (hidden + mixed).astype(BF).reshape(NZ, BLK, CHUNK)
        done = lax.all_to_all(done, "z", split_axis=0, concat_axis=0, tiled=True)
        return done.transpose(1, 0, 2).reshape(BLK, D)


def solution(mesh):
    fine = Mesh(mesh.devices.reshape(NY, NX, NZ, 2), ("y", "x", "z", "core"))
    ctx, head = ("y", "x"), ("z", "core")
    both = ctx + head
    in_specs = (
        P(both, None, None),
        P(ctx, None),
        P(head, None, None),
        P(head, None, None),
        P(head, None),
        P(both, None),
        P(),
        P(both, None),
        P(both, None),
        P(),
        P(ctx, None, head),
        P(ctx, None, head),
        P(ctx, head, None),
    )
    return jax.shard_map(shards, mesh=fine, in_specs=in_specs, out_specs=P(both, None), check_vma=False)
```

```python
import functools

import jax
import jax.numpy as jnp
from jax import lax
from jax.experimental import pallas as pl
from jax.experimental.pallas import tpu as pltpu
from jax.sharding import Mesh
from jax.sharding import PartitionSpec as P

D = 7168
NOPE = 128
ROPE = 64
LAT = 512
VDIM = 128
EXPERTS = 16
TOP = 8
RESP = 1024
PROMPT = 7168
NX = 4
NY = 4
NZ = 4
GRP = 8
BLK = 8
CAP = 6
QCOLS = GRP * (NOPE + ROPE) + 128
KEYS = 2048
HALF = 256
ROWS = 256
CHUNK = D // NZ
SLOTS = NZ * CAP
EROWS = 16 * SLOTS
LOG2E = 1.4426950408889634
BF = jnp.bfloat16
F32 = jnp.float32
HIDE = -1e30


def shift(a, axis, n, d):
    return lax.ppermute(a, axis, [(i, (i + d) % n) for i in range(n)])


def split3(v):
    hi = v.astype(BF).astype(F32)
    mid = (v - hi).astype(BF).astype(F32)
    low = (v - hi - mid).astype(BF).astype(F32)
    return hi, mid, low


def cost(flops=0, nbytes=1):
    return pl.CostEstimate(flops=flops, bytes_accessed=nbytes, transcendentals=0)


def call(kernel, name, out_shape, in_specs, scratch, mib=32, **more):
    return pl.pallas_call(
        kernel,
        out_shape=out_shape,
        in_specs=in_specs,
        scratch_shapes=scratch,
        compiler_params=pltpu.CompilerParams(vmem_limit_bytes=mib * 2**20),
        cost_estimate=cost(),
        name=name,
        **more,
    )


VM = pl.BlockSpec(memory_space=pltpu.VMEM)
SM = pl.BlockSpec(memory_space=pltpu.SMEM)
AT = pl.BlockSpec(memory_space=pltpu.HBM)
PAIR = 2


def attention_kernel(
    pos_ref, q_ref, first_ref, last_ref, c0, c1, c2, c3, s1, s2, s3, ak_ref, av_ref, o0, o1, o2, o3, kv, rp, st, hide, sem
):
    g = pl.program_id(0)
    outs = (o0, o1, o2, o3)

    def query(at):
        blocks = [lax.rem(pos_ref[7] + d, NY) for d in range(NY)]
        return jnp.concatenate([q_ref[b, :, pl.ds(pl.multiple_of(at, 128), 128)] for b in blocks], axis=0)

    @pl.when(g == 0)
    def _():
        copies = [pltpu.make_async_copy(c0, kv.at[pl.ds(pl.multiple_of(pos_ref[0], HALF), 2 * HALF)], sem.at[0])]
        for i, piece in enumerate((c1, c2, c3, s1, s2, s3)):
            to = kv.at[pl.ds(pl.multiple_of(pos_ref[1 + i], HALF), HALF)]
            copies.append(pltpu.make_async_copy(piece, to, sem.at[1 + i]))
        for c in copies:
            c.start()
        col = lax.broadcasted_iota(jnp.int32, (ROWS, KEYS // 2), 1)
        hide[...] = jnp.where((col >= first_ref[...]) & (col <= last_ref[...]), 0.0, HIDE)
        st[...] = jnp.zeros_like(st)
        for c in copies:
            c.wait()
        r = kv[:, LAT:]
        rp[...] = jnp.concatenate([r, r], axis=1)

    lane = lax.broadcasted_iota(jnp.int32, (ROWS, 128), 1)
    nt = (((1,), (1,)), ((), ()))
    step = 512
    scale = LOG2E * (NOPE + ROPE) ** (-0.5)
    scored = []
    for i in range(PAIR):
        h = g * PAIR + i
        nope = query(h * NOPE)
        q_lat = jnp.dot(nope, ak_ref[i], preferred_element_type=F32).astype(BF)
        pair = query(GRP * NOPE + (h // 2) * 128).astype(F32)
        rope = jnp.where(lane // ROPE == h % 2, pair, 0.0).astype(BF)
        parts = []
        for j in range(0, KEYS, step):
            s = lax.dot_general(q_lat, kv[j : j + step, :LAT], nt, preferred_element_type=F32)
            s = s + lax.dot_general(rope, rp[j : j + step, :], nt, preferred_element_type=F32)
            if j >= KEYS // 2:
                s = s + hide[:, j - KEYS // 2 : j - KEYS // 2 + step]
            parts.append(s)
        scored.append(parts)
    for i, parts in enumerate(scored):
        h = g * PAIR + i
        top = jnp.max(parts[0], axis=1, keepdims=True)
        for s in parts[1:]:
            top = jnp.maximum(top, jnp.max(s, axis=1, keepdims=True))
        total = jnp.zeros((ROWS, 1), F32)
        acc = jnp.zeros((ROWS, LAT), F32)
        for n, s in enumerate(parts):
            p = jnp.exp2((s - top) * scale)
            total = total + jnp.sum(p, axis=1, keepdims=True)
            acc = acc + jnp.dot(p.astype(BF), kv[n * step : (n + 1) * step, :LAT], preferred_element_type=F32)
        lat = (acc / total).astype(BF)
        head = jnp.dot(lat, av_ref[i], preferred_element_type=F32).astype(BF)
        for d, o in enumerate(outs):
            o[:, pl.ds(pl.multiple_of(h * VDIM, VDIM), VDIM)] = head[d * 64 : (d + 1) * 64]
        add = jnp.zeros((ROWS, 128), F32)
        for n, v in enumerate(split3(top) + split3(total)):
            add = add + jnp.where(lane == n * GRP + h, v, 0.0)
        st[...] += add

    @pl.when(g == GRP // PAIR - 1)
    def _():
        for d, o in enumerate(outs):
            o[:, GRP * VDIM :] = st[d * 64 : (d + 1) * 64, :].astype(BF)


def attention(place, q, first, last, pieces, absorb_key, absorb_value):
    whole = lambda a: pl.BlockSpec(a.shape, lambda g: (0,) * a.ndim)
    return call(
        attention_kernel,
        "attention",
        (jax.ShapeDtypeStruct((64, GRP * VDIM + 128), BF),) * NY,
        [SM, whole(q), whole(first), whole(last)]
        + [AT] * 7
        + [
            pl.BlockSpec((PAIR, NOPE, LAT), lambda g: (g, 0, 0)),
            pl.BlockSpec((PAIR, LAT, VDIM), lambda g: (g, 0, 0)),
        ],
        [
            pltpu.VMEM((KEYS, LAT + ROPE), BF),
            pltpu.VMEM((KEYS, 2 * ROPE), BF),
            pltpu.VMEM((ROWS, 128), F32),
            pltpu.VMEM((ROWS, KEYS // 2), F32),
            pltpu.SemaphoreType.DMA((7,)),
        ],
        grid=(GRP // PAIR,),
        out_specs=(pl.BlockSpec((64, GRP * VDIM + 128), lambda g: (0, 0)),) * NY,
    )(place, q, first, last, *pieces, absorb_key, absorb_value)


def routing_kernel(at_ref, col_ref, q_ref, pick_ref, blend_ref, held, sem):
    rows = q_ref.at[pl.ds(pl.multiple_of(at_ref[0], NZ * BLK), NZ * BLK), pl.ds(QCOLS - 128, 128)]
    copy = pltpu.make_async_copy(rows, held, sem)
    copy.start()
    copy.wait()
    info = held[...].astype(F32)
    rows = NZ * BLK
    route = info[:, :TOP]
    score = info[:, TOP : 2 * TOP] + info[:, 2 * TOP : 3 * TOP] + info[:, 3 * TOP : 4 * TOP]
    weight = 2.5 * score / jnp.sum(score, axis=1, keepdims=True)
    expert, block, slot = col_ref[0:1, :], col_ref[1:2, :], col_ref[2:3, :]
    named = jnp.zeros((rows, EROWS), F32)
    mix = jnp.zeros((rows, EROWS), F32)
    for n in range(TOP):
        hit = route[:, n : n + 1] == expert
        named = named + jnp.where(hit, 1.0, 0.0)
        mix = mix + jnp.where(hit, weight[:, n : n + 1], 0.0)
    i = lax.broadcasted_iota(jnp.int32, (rows, rows), 0)
    j = lax.broadcasted_iota(jnp.int32, (rows, rows), 1)
    ahead = jnp.where((j < i) & (j // BLK == i // BLK), 1.0, 0.0).astype(BF)
    rank = jnp.dot(ahead, named.astype(BF), preferred_element_type=F32)
    mine = (lax.broadcasted_iota(jnp.int32, (rows, EROWS), 0) // BLK).astype(F32)
    place = (named > 0.5) & (block == mine) & (slot == rank)
    pick_ref[...] = jnp.where(place, 1.0, 0.0).astype(BF)
    blend_ref[...] = jnp.where(place, mix, 0.0)


def routing(at, q):
    col = jnp.arange(EROWS, dtype=jnp.int32)
    cols = jnp.stack([col // SLOTS, col % SLOTS // CAP, col % CAP] + [col * 0] * 5).astype(F32)
    rows = NZ * BLK
    return call(
        routing_kernel,
        "routing",
        (jax.ShapeDtypeStruct((rows, EROWS), BF), jax.ShapeDtypeStruct((rows, EROWS), F32)),
        [SM, VM, AT],
        [pltpu.VMEM((rows, 128), BF), pltpu.SemaphoreType.DMA],
        out_specs=(VM, VM),
    )(at, cols, q)


def merge_kernel(o0, o1, o2, o3, head_out):
    outs = (o0, o1, o2, o3)
    tops, totals = [], []
    for o in outs:
        st = o[:, GRP * VDIM :].astype(F32)
        part = [st[:, n * GRP : (n + 1) * GRP] for n in range(6)]
        tops.append(part[0] + part[1] + part[2])
        totals.append(part[3] + part[4] + part[5])
    top = jnp.maximum(jnp.maximum(tops[0], tops[1]), jnp.maximum(tops[2], tops[3]))
    scale = LOG2E * (NOPE + ROPE) ** (-0.5)
    share = [t * jnp.exp2((m - top) * scale) for m, t in zip(tops, totals)]
    whole = share[0] + share[1] + share[2] + share[3]
    share = [s / whole for s in share]
    for h in range(GRP):
        at = slice(h * VDIM, (h + 1) * VDIM)
        total = sum(o[:, at].astype(F32) * share[s][:, h : h + 1] for s, o in enumerate(outs))
        head_out[:, at] = total.astype(BF)


def merge(outs):
    return call(
        merge_kernel,
        "merge",
        jax.ShapeDtypeStruct((64, GRP * VDIM), BF),
        [VM] * 4,
        [],
        out_specs=VM,
    )(*outs)


def stage_kernel(token_ref, w_ref, held_ref, sem):
    rows = w_ref.shape[0] // 8
    copies = [
        pltpu.make_async_copy(w_ref.at[pl.ds(i * rows, rows)], held_ref.at[pl.ds(i * rows, rows)], sem.at[i])
        for i in range(8)
    ]
    for c in copies:
        c.start()
    for c in copies:
        c.wait()


def stage(token, w):
    return call(
        stage_kernel,
        "stage",
        pltpu.VMEM(w.shape, w.dtype),
        [AT, AT],
        [pltpu.SemaphoreType.DMA((8,))],
        mib=44,
        out_specs=VM,
    )(token, w)


def project_kernel(ways, own_ref, head_ref, w_ref, res_ref, *outs):
    half = NZ * BLK
    for n, d in enumerate(ways):
        keep_ref, send_ref = outs[2 * n], outs[2 * n + 1]
        at = pl.ds(pl.multiple_of(lax.rem(own_ref[1] + d, NZ) * CHUNK, CHUNK), CHUNK)
        part = jnp.dot(head_ref[...], w_ref[:, at], preferred_element_type=F32)
        row = lax.broadcasted_iota(jnp.int32, part.shape, 0) // BLK
        res = jnp.concatenate([res_ref[:, at].astype(F32)] * 8, axis=0)
        part = part + jnp.where(row == own_ref[0] * NZ + own_ref[1], res, 0.0)
        low = jnp.broadcast_to(own_ref[0], (half, CHUNK)) == 0
        keep_ref[...] = jnp.where(low, part[:half], part[half:])
        send_ref[...] = jnp.where(low, part[half:], part[:half]).astype(BF)


def project(ways, own, head_out, out_proj, residual):
    shape = (NZ * BLK, CHUNK)
    return call(
        functools.partial(project_kernel, ways),
        "project",
        (jax.ShapeDtypeStruct(shape, F32), jax.ShapeDtypeStruct(shape, BF)) * len(ways),
        [SM] + [VM] * 3,
        [],
        out_specs=(VM,) * (2 * len(ways)),
    )(own, head_out, out_proj, residual)


def fold_kernel(n, *refs):
    for keep, got, out in zip(refs[:n], refs[n : 2 * n], refs[2 * n :]):
        out[...] = (keep[...] + got[...].astype(F32)).astype(BF)


def fold(keeps, gots):
    n = len(keeps)
    return call(
        functools.partial(fold_kernel, n),
        "fold",
        (jax.ShapeDtypeStruct((NZ * BLK, CHUNK), BF),) * n,
        [VM] * (2 * n),
        [],
        out_specs=(VM,) * n,
    )(*keeps, *gots)


def spread_kernel(keep_ref, got_ref, p1, p2, p3, gain_ref, pick_ref, hidden_ref, rows_ref):
    hidden = keep_ref[...] + got_ref[...].astype(F32) + p1[...].astype(F32) + p2[...].astype(F32) + p3[...].astype(F32)
    hidden_ref[...] = hidden
    scaled = (hidden * gain_ref[...]).astype(BF)
    tn = (((0,), (0,)), ((), ()))
    rows_ref[...] = lax.dot_general(pick_ref[...], scaled, tn, preferred_element_type=F32).astype(BF)


def spread(parts, gain, pick):
    return call(
        spread_kernel,
        "spread",
        (jax.ShapeDtypeStruct((NZ * BLK, CHUNK), F32), pltpu.VMEM((EROWS, CHUNK), BF)),
        [VM] * 7,
        [],
        out_specs=(VM, VM),
    )(*parts, gain, pick)


def gather_kernel(*refs):
    pieces, (held_ref, sem) = refs[:8], refs[8:]
    n = pieces[0].shape[0]
    copies = [pltpu.make_async_copy(p, held_ref.at[pl.ds(i * n, n)], sem.at[i]) for i, p in enumerate(pieces)]
    for c in copies:
        c.start()
    for c in copies:
        c.wait()


def gather(pieces):
    return call(
        gather_kernel,
        "down_weights",
        pltpu.VMEM((1024, CHUNK), BF),
        [AT] * 8,
        [pltpu.SemaphoreType.DMA((8,))],
        mib=16,
        out_specs=VM,
    )(*pieces)


def gate_up_kernel(z_ref, x_ref, gain_ref, *refs):
    pieces, (o_ref, w, sem) = refs[:8], refs[8:]
    copies = [
        pltpu.make_async_copy(p, w.at[:, pl.ds(i * 256, 256)], sem.at[i]) for i, p in enumerate(pieces)
    ]
    for c in copies:
        c.start()
    x = x_ref[...]
    raw = x.astype(F32) * gain_ref[...]
    ones = jnp.ones((8, CHUNK), BF)
    square = lax.dot_general(
        ones, (raw * raw).astype(BF), (((1,), (1,)), ((), ())), preferred_element_type=F32
    )
    row = lax.broadcasted_iota(jnp.int32, square.shape, 0)
    hi, mid, low = split3(square)
    coded = jnp.where(row == 0, hi, jnp.where(row == 1, mid, jnp.where(row == 2, low, 0.0)))
    coded = jnp.concatenate([coded, jnp.zeros_like(coded)], axis=0).astype(BF)
    coded = jnp.concatenate([coded, jnp.zeros((16, 512 - EROWS), BF)], axis=1)
    for d in range(NZ):
        copies[2 * d].wait()
        copies[2 * d + 1].wait()
        part = jnp.dot(x, w[:, d * 512 : (d + 1) * 512], preferred_element_type=F32).astype(BF)
        to = lax.rem(z_ref[0] + NZ - d, NZ)
        o_ref[to, :EROWS] = part
        o_ref[to, EROWS:] = coded


def gate_up(z, x, gain, pieces):
    return call(
        gate_up_kernel,
        "gate_up",
        pltpu.VMEM((NZ, EROWS + 16, 512), BF),
        [SM, VM, VM] + [AT] * 8,
        [pltpu.VMEM((CHUNK, 2048), BF), pltpu.SemaphoreType.DMA((8,))],
        mib=56,
        out_specs=VM,
    )(z, x, gain, *pieces)


def inner_kernel(part_ref, out_ref):
    total = part_ref[0].astype(F32)
    for s in range(1, NZ):
        total = total + part_ref[s].astype(F32)
    square = jnp.sum(total[EROWS : EROWS + 8], axis=0, keepdims=True)
    scale = lax.rsqrt(jnp.broadcast_to(square[:, :EROWS], (8, EROWS)) / D + 1e-6).T[:, :1]
    total = total[:EROWS] * scale
    for k in range(2):
        gate, up = total[:, k * 256 : k * 256 + 128], total[:, k * 256 + 128 : k * 256 + 256]
        out_ref[:, k * 128 : (k + 1) * 128] = (gate / (1.0 + jnp.exp(-gate)) * up).astype(BF)


def inner_act(part):
    return call(inner_kernel, "inner_act", jax.ShapeDtypeStruct((EROWS, 256), BF), [VM], [], out_specs=VM)(part)


def down_kernel(i0, i1, i2, i3, w, o_ref):
    inner = jnp.concatenate([i0[...], i1[...], i2[...], i3[...]], axis=1)
    o_ref[...] = jnp.dot(inner, w[...], preferred_element_type=F32).astype(BF)


def down(inners, held):
    return call(
        down_kernel,
        "down",
        pltpu.VMEM((EROWS, CHUNK), BF),
        [VM] * 5,
        [],
        out_specs=VM,
    )(*inners, held)


def after(arrays, token):
    out = lax.optimization_barrier(tuple(arrays) + (token,))
    return out[:-1]


def turned(a, by):
    return lax.dynamic_slice_in_dim(jnp.concatenate([a, a]), by, a.shape[0], axis=0).reshape(-1)


def shards(
    queries,
    latent_cache,
    absorb_key,
    absorb_value,
    out_proj,
    residual,
    norm_gain,
    routes,
    route_score,
    response_doc,
    expert_gate,
    expert_up,
    expert_down,
):
    x, y, z, k = (lax.axis_index(a) for a in ("x", "y", "z", "core"))

    with jax.named_scope("cache_gather"):
        half = lax.dynamic_slice_in_dim(latent_cache, k * HALF, HALF, axis=0)
        mine = [shift(half, "x", NX, d) for d in range(1, NX)]

    with jax.named_scope("query_exchange"):
        score_hi = lax.reduce_precision(route_score, 8, 7)
        score_mid = lax.reduce_precision(route_score - score_hi, 8, 7)
        score_low = route_score - score_hi - score_mid
        info = jnp.concatenate(
            [routes.astype(BF)]
            + [s.astype(BF) for s in (score_hi, score_mid, score_low)]
            + [jnp.zeros((BLK, 128 - 4 * TOP), BF)],
            axis=1,
        )
        info = jnp.broadcast_to(info[:, None, None], (BLK, NZ, 2, 128))
        nope = queries[:, :, :NOPE].reshape(BLK, NZ, 2, GRP * NOPE)
        rope = queries[:, :, NOPE:].reshape(BLK, NZ, 2, GRP * ROPE)
        q = jnp.concatenate([nope, rope, info], axis=3).transpose(2, 1, 0, 3)
        q = jnp.broadcast_to(q[None], (NY, 2, NZ, BLK, QCOLS))
        q = q.reshape(NY * 2 * NZ, BLK, QCOLS)
        (q,) = after([q], mine[0])
        q = lax.all_to_all(q, ("y", "core", "z"), split_axis=0, concat_axis=0, tiled=True)
        q = q.reshape(ROWS, QCOLS)

    with jax.named_scope("weights"):
        gates = expert_gate[0].reshape(NZ, CHUNK, 128)
        ups = expert_up[0].reshape(NZ, CHUNK, 128)
        downs = expert_down[0]
        gu, dn = [], []
        for d in range(NZ):
            to = (z + d) % NZ
            g = lax.dynamic_index_in_dim(gates, to, 0, keepdims=False)
            u = lax.dynamic_index_in_dim(ups, to, 0, keepdims=False)
            gu.append(jnp.concatenate([g, u], axis=1))
            dn.append(lax.dynamic_slice_in_dim(downs, to * CHUNK, CHUNK, axis=1))
    with jax.named_scope("cache_share"):
        other = [shift(m, "core", 2, 1) for m in mine]

    with jax.named_scope("attention"):
        doc = lax.dynamic_index_in_dim(response_doc.reshape(NY, NX, NZ, 2, BLK), x, 1, keepdims=False)
        doc = turned(doc.transpose(0, 2, 1, 3).reshape(NY, 64), y)
        ids = jnp.arange(RESP, dtype=jnp.int32).reshape(NY, NX, NZ, 2, BLK)
        ids = lax.dynamic_index_in_dim(ids, x, 1, keepdims=False).transpose(0, 2, 1, 3).reshape(NY, 64)
        ids = turned(ids, y)
        start = jnp.sum((response_doc[None, :] < doc[:, None]).astype(jnp.int32), axis=1)
        far = jnp.int32(1 << 20)
        first = jnp.where(y == NY - 1, start, -far)[:, None]
        last = jnp.where(y == NY - 1, ids, far)[:, None]
        at = [x * 512]
        for core in (k, 1 - k):
            at += [((x - d) % NX) * 512 + core * HALF for d in range(1, NX)]
        place_of = jnp.stack(at + [y]).astype(jnp.int32)

        ahead = after(gu[1:], q)
        q, *dn = lax.optimization_barrier((q, *dn))
        gu = gu[:1] + [shift(w, "z", NZ, d + 1) for d, w in enumerate(ahead)]
        outs = attention(place_of, q.reshape(NY, 64, QCOLS), first, last, [latent_cache] + mine + other, absorb_key, absorb_value)

    with jax.named_scope("combine"):
        held = stage(outs[0], out_proj)
        outs = [outs[0]] + [shift(o, "y", NY, d + 1) for d, o in enumerate(outs[1:])]

    with jax.named_scope("routing"):
        pick, blend = routing(((y * 2 + k) * NZ * BLK).reshape(1), after([q], outs[0])[0])

    with jax.named_scope("out_projection"):
        own = jnp.stack([k, z])
        head_out = merge(outs)
        keep1, send1, keep2, send2 = project((1, 2), own, head_out, held, residual)
        swap1 = [shift(a, "core", 2, 1) for a in (send1, send2)]
        (head_out,) = after([head_out], send1)
        keep3, send3, keep, send = project((3, 0), own, head_out, held, residual)
        swap2 = [shift(a, "core", 2, 1) for a in (send3, send)]
        keep, *moved = lax.optimization_barrier((keep, *gu[1:]))
        gu = gu[:1] + list(moved)
        part1, part2 = fold([keep1, keep2], swap1)
        (part3,) = fold([keep3], swap2[:1])
        sums = part3
        parts = [shift(p, "z", NZ, d + 1) for d, p in enumerate((part1, part2, part3))]
        parts = [keep, swap2[1]] + parts

    with jax.named_scope("dispatch"):
        gain = lax.dynamic_slice_in_dim(norm_gain, z * CHUNK, CHUNK)[None]
        gu_other = [shift(w, "core", 2, 1) for w in after(gu, keep)]
        hidden, rows = spread(parts, gain, pick)
        ahead = after(dn[1:], sums)
        dn = dn[:1] + [shift(w, "z", NZ, d + 1) for d, w in enumerate(ahead)]
        rows = rows.reshape(EXPERTS, SLOTS, CHUNK)
        rows = lax.all_to_all(rows, ("y", "x"), split_axis=0, concat_axis=0, tiled=True)
        rows = rows.reshape(EROWS, CHUNK)

    with jax.named_scope("experts"):
        rows, *gu_other = lax.optimization_barrier((rows, *gu_other))
        part = gate_up(z.reshape(1), rows, 1.0 / gain, [w for pair in zip(gu, gu_other) for w in pair])
        part, *moved = lax.optimization_barrier((part, *dn[1:]))
        dn = dn[:1] + list(moved)
        dn_other = [shift(w, "core", 2, 1) for w in after(dn, part)]
        part = lax.all_to_all(part, "z", split_axis=0, concat_axis=0, tiled=True)
        inner = inner_act(part)
        inners = [inner] + [shift(inner, "z", NZ, d) for d in range(1, NZ)]
        held = gather([w for pair in zip(dn, dn_other) for w in pair])
        result = down(inners, held)

    with jax.named_scope("return"):
        back = lax.all_to_all(
            result.reshape(EXPERTS, SLOTS, CHUNK), ("y", "x"), split_axis=0, concat_axis=0, tiled=True
        ).reshape(EROWS, CHUNK)
        mixed = jnp.dot(blend, back.astype(F32), precision=lax.Precision.HIGHEST, preferred_element_type=F32)
        done = (hidden + mixed).astype(BF).reshape(NZ, BLK, CHUNK)
        done = lax.all_to_all(done, "z", split_axis=0, concat_axis=0, tiled=True)
        return done.transpose(1, 0, 2).reshape(BLK, D)


def solution(mesh):
    fine = Mesh(mesh.devices.reshape(NY, NX, NZ, 2), ("y", "x", "z", "core"))
    ctx, head = ("y", "x"), ("z", "core")
    both = ctx + head
    in_specs = (
        P(both, None, None),
        P(ctx, None),
        P(head, None, None),
        P(head, None, None),
        P(head, None),
        P(both, None),
        P(),
        P(both, None),
        P(both, None),
        P(),
        P(ctx, None, head),
        P(ctx, None, head),
        P(ctx, head, None),
    )
    return jax.shard_map(shards, mesh=fine, in_specs=in_specs, out_specs=P(both, None), check_vma=False)
```
